32 devices in a mesh: dp: 8 (over z, x), pipe: 2 (over y), tensor: 2 (over core).
Axes of the slice: x: 2, y: 2, z: 4, core: 2. Of those that a mesh axis runs over, the one named last changes fastest.
Arguments:
- query_states: bfloat16 [2, 512, 4096], P('pipe', 'dp', 'tensor'), may hold values from -6 to 6
- passage_hidden_states: bfloat16 [2, 1440, 4096], P('pipe', 'dp', 'tensor'), may hold values from -6 to 6
- w_query: bfloat16 [2, 4096, 4096], P('pipe', 'dp', 'tensor'), may hold values from -0.09375 to 0.09375
- key_matrix: bfloat16 [2, 4096, 1024], P('pipe', 'dp', 'tensor'), may hold values from -0.09375 to 0.09375
- value_matrix: bfloat16 [2, 4096, 1024], P('pipe', 'dp', 'tensor'), may hold values from -0.09375 to 0.09375
- w_out: bfloat16 [2, 4096, 4096], P('pipe', 'tensor', 'dp'), may hold values from -0.09375 to 0.09375
- final_gain: bfloat16 [4096], P('tensor'), may hold values from 0.5 to 2
- w_vector: bfloat16 [4096, 128], P('tensor'), may hold values from -0.09375 to 0.09375
- lengths: int32 [8], P('dp'), may hold values from 1 to 180, 896 in all
- teacher: float32 [16, 8], P(('dp', 'pipe')), may hold values from -12 to 12
Outputs:
- boundary_queries: bfloat16 [2, 512, 4096], P('pipe', 'dp', 'tensor')
- boundary_passages: bfloat16 [2, 1440, 4096], P('pipe', 'dp', 'tensor')
- scores: float32 [16, 8], P(('dp', 'pipe'))
- divergence: float32 [16], P(('dp', 'pipe'))
The draws below stay inside these ranges and needn't reach their ends.
Inputs may be any that keep to these rules, and one draw needn't show every extreme that they name: Each passage's valid tokens come first; slots after lengths[p] are padding. Some passage fills all 180 slots.
All inputs are finite; a program needn't handle non-finite values. No bound on the sum of `lengths` on one device may be relied on, other than what follows from the above.
Results may differ from the reference program's by a relative error of at most 0.0075.
Values may be sent and summed in bfloat16 or wider, within the bound.
A program may use at most 128 MiB of HBM per device.

```python
import math
import jax
import jax.numpy as jnp
import numpy as np
from jax import lax

MODEL_WIDTH = 4096
HQ = 32
KEY_VALUE_HEADS = 8
HEAD_WIDTH = 128
VEC = 128
QLEN = 32
PLEN = 180
RELAY_SECTIONS = 2
QUERIES = 16
PASSAGES = 8
N_TENSOR = 2


def block_scale(rng, extent, split, smallest, largest):
    def one(position, parts):
        steps = jax.random.uniform(jax.random.fold_in(jax.random.fold_in(rng, 6), position), (parts,), jnp.float32, smallest / len(split), largest / len(split))
        return jnp.repeat(jnp.exp(steps), extent[position] // parts).reshape((-1,) + (1,) * (len(extent) - position - 1))

    gain = one(*split[0])
    for cut in split[1:]:
        gain = gain * one(*cut)
    return gain


def split_up(number_of, total, most, slope):
    weights = [(1 << 20) // math.isqrt(standing ** slope) + 1 for standing in range(2, number_of + 1)]
    rest, given = total - most - (number_of - 1), [1] * (number_of - 1)
    while rest > 0:
        free = [i for i in range(number_of - 1) if given[i] < most]
        pool, budget = sum([weights[i] for i in free]), rest
        for i in free:
            addition = min(most - given[i], max(1, budget * weights[i] // pool), rest)
            given[i] = given[i] + addition
            rest = rest - addition
    return np.array([most] + given)


def ragged(rng, amount, total, limit, lean):
    if amount == 2:
        one = jax.random.randint(rng, (), max(1, total - limit), min(limit, total - 1) + 1)
        return jnp.stack([one, total - one])
    tallies = jnp.asarray(split_up(amount, total, limit, lean), jnp.int32)
    pairs = (amount - 1) // 2
    donor, sink = tallies[1:1 + 2 * pairs:2], tallies[2:2 + 2 * pairs:2]
    slack = jnp.minimum(donor - 1, limit - sink)
    passed = jax.random.randint(jax.random.fold_in(rng, 1), (pairs,), 0, 1 << 20) % (slack + 1)
    tallies = tallies.at[1:1 + 2 * pairs:2].set(donor - passed).at[2:2 + 2 * pairs:2].set(sink + passed)
    return tallies[jax.random.permutation(jax.random.fold_in(rng, 2), amount)]


def gaussian(rng, shape, scale, limit, shards=(), held_as=jnp.bfloat16):
    array = scale * jax.random.normal(rng, shape, jnp.float32)
    if shards:
        array = array * block_scale(rng, shape, shards, -0.22, 0.18)
    return jnp.clip(array, -limit, limit).astype(held_as)


def setup_inputs(seed: int = 0) -> dict:
    seeds = jax.random.split(jax.random.key(seed), 11)
    return {
        "query_states": gaussian(seeds[0], (RELAY_SECTIONS, QUERIES * QLEN, MODEL_WIDTH), 1.0, 6.0, ((0, 2), (1, 8), (2, 2))),
        "passage_hidden_states": gaussian(seeds[1], (RELAY_SECTIONS, PASSAGES * PLEN, MODEL_WIDTH), 1.0, 6.0, ((0, 2), (1, 8), (2, 2))),
        "w_query": gaussian(seeds[2], (RELAY_SECTIONS, MODEL_WIDTH, HQ * HEAD_WIDTH), MODEL_WIDTH ** -0.5, 0.09375, ((0, 2), (1, 8), (2, 2))),
        "key_matrix": gaussian(seeds[3], (RELAY_SECTIONS, MODEL_WIDTH, KEY_VALUE_HEADS * HEAD_WIDTH), MODEL_WIDTH ** -0.5, 0.09375, ((0, 2), (1, 8), (2, 2))),
        "value_matrix": gaussian(seeds[4], (RELAY_SECTIONS, MODEL_WIDTH, KEY_VALUE_HEADS * HEAD_WIDTH), MODEL_WIDTH ** -0.5, 0.09375, ((0, 2), (1, 8), (2, 2))),
        "w_out": gaussian(seeds[5], (RELAY_SECTIONS, HQ * HEAD_WIDTH, MODEL_WIDTH), (HQ * HEAD_WIDTH) ** -0.5, 0.09375, ((0, 2), (1, 2), (2, 8))),
        "final_gain": jnp.clip(jnp.exp(math.log(2.0) - 1.3862944 * jax.random.uniform(seeds[6], (MODEL_WIDTH,), jnp.float32) ** block_scale(seeds[6], (MODEL_WIDTH,), ((0, 2),), -0.2, 0.2)), 0.5, 2.0).astype(jnp.bfloat16),
        "w_vector": gaussian(seeds[7], (MODEL_WIDTH, VEC), MODEL_WIDTH ** -0.5, 0.09375, ((0, 2),)),
        "lengths": ragged(seeds[8], PASSAGES, PASSAGES * (PLEN * 5 // 8), PLEN, 2).astype(jnp.int32),
        "teacher": gaussian(seeds[9], (QUERIES, PASSAGES), 3.0, 12.0, ((0, 16),), jnp.float32),
    }


norm_epsilon = 1e-05
vector_epsilon = 1e-06
rope_base = 10000.0

def rotate(values_in, positions):
    half_size = values_in.shape[-1] // 2
    frequency = rope_base ** (-jnp.arange(half_size).astype(jnp.float32) / half_size)
    angles = positions.astype(jnp.float32)[:, None] * frequency[None, :]
    cosine = jnp.cos(angles)[:, None, :]
    sine = jnp.sin(angles)[:, None, :]
    first_half = values_in[..., :half_size]
    second_half = values_in[..., half_size:]
    return jnp.concatenate([first_half * cosine - second_half * sine, second_half * cosine + first_half * sine], axis=-1)

def attend(queries, keys, values_in):
    batch_count, length, head_count, head_size = queries.shape
    key_heads = keys.shape[2]
    grouped = queries.reshape(batch_count, length, key_heads, head_count // key_heads, head_size)
    logits = jnp.einsum('bskgd,bukd->bkgsu', grouped.astype(jnp.float32), keys.astype(jnp.float32)) * head_size ** (-0.5)
    causal = jnp.arange(length)[:, None] >= jnp.arange(length)[None, :]
    weights = jnp.where(causal, jnp.exp(logits), 0.0)
    probability = (weights / lax.optimization_barrier(jnp.sum(weights, axis=-1, keepdims=True))).astype(jnp.bfloat16)
    combined = jnp.einsum('bkgsu,bukd->bskgd', probability.astype(jnp.float32), values_in.astype(jnp.float32))
    return combined.reshape(batch_count * length, head_count * head_size).astype(jnp.bfloat16)

def by_sequence(array_in, head_number, seq_length):
    return array_in.reshape(-1, seq_length, head_number, HEAD_WIDTH)

def layer(query_rows, passage_rows, w_query, key_matrix, value_matrix, w_out):
    query_count = query_rows.shape[0]
    joined = jnp.concatenate([query_rows, passage_rows], axis=0)
    widened = joined.astype(jnp.float32)
    normed = (widened * lax.rsqrt(lax.optimization_barrier(jnp.mean(widened * widened, axis=1, keepdims=True)) + norm_epsilon)).astype(jnp.bfloat16)
    queries = jnp.dot(normed, w_query, preferred_element_type=jnp.float32)
    keys = jnp.dot(normed, key_matrix, preferred_element_type=jnp.float32)
    values_out = jnp.dot(normed, value_matrix, preferred_element_type=jnp.float32).astype(jnp.bfloat16)
    query_heads = w_query.shape[1] // HEAD_WIDTH
    key_heads = key_matrix.shape[1] // HEAD_WIDTH
    query_pos = jnp.arange(QLEN)
    passage_pos = jnp.arange(PLEN)
    short_q = rotate(by_sequence(queries[:query_count], query_heads, QLEN), query_pos).astype(jnp.bfloat16)
    short_k = rotate(by_sequence(keys[:query_count], key_heads, QLEN), query_pos).astype(jnp.bfloat16)
    short_v = by_sequence(values_out[:query_count], key_heads, QLEN)
    long_q = rotate(by_sequence(queries[query_count:], query_heads, PLEN), passage_pos).astype(jnp.bfloat16)
    long_k = rotate(by_sequence(keys[query_count:], key_heads, PLEN), passage_pos).astype(jnp.bfloat16)
    long_v = by_sequence(values_out[query_count:], key_heads, PLEN)
    attended = jnp.concatenate([attend(short_q, short_k, short_v), attend(long_q, long_k, long_v)], axis=0)
    group_cols = attended.shape[1] // N_TENSOR
    branch = jnp.zeros((joined.shape[0], w_out.shape[1]), jnp.float32)
    for group in range(N_TENSOR):
        lower = group * group_cols
        upper = lower + group_cols
        term = jnp.dot(attended[:, lower:upper], w_out[lower:upper], preferred_element_type=jnp.float32).astype(jnp.bfloat16)
        branch = branch + lax.optimization_barrier(term).astype(jnp.float32)
    updated = (widened + branch).astype(jnp.bfloat16)
    return (updated[:query_count], updated[query_count:])

def late_scores(query_vectors, passage_vectors, passage_lengths):
    sims = jnp.einsum('qtc,psc->qtps', query_vectors.astype(jnp.float32), passage_vectors.astype(jnp.float32))
    valid = jnp.arange(passage_vectors.shape[1])[None, :] < passage_lengths[:, None]
    masked = jnp.where(valid[None, None], sims, -3.0)
    return lax.optimization_barrier(jnp.sum(lax.optimization_barrier(jnp.max(masked, axis=3)), axis=1))

def divergence_rows(student, teacher_rows):
    log_student = student - jnp.log(lax.optimization_barrier(jnp.sum(jnp.exp(student), axis=1, keepdims=True)))
    log_teacher = teacher_rows - jnp.log(lax.optimization_barrier(jnp.sum(jnp.exp(teacher_rows), axis=1, keepdims=True)))
    return lax.optimization_barrier(jnp.sum(jnp.exp(log_teacher) * (log_teacher - log_student), axis=1))

def reference(query_states, passage_hidden_states, w_query, key_matrix, value_matrix, w_out, final_gain, w_vector, lengths, teacher):
    query_outs = []
    passage_outs = []
    for section in range(RELAY_SECTIONS):
        new_query, new_passage = layer(query_states[section], passage_hidden_states[section], w_query[section], key_matrix[section], value_matrix[section], w_out[section])
        query_outs.append(new_query)
        passage_outs.append(new_passage)
    boundary_queries = jnp.stack(query_outs, axis=0)
    boundary_passages = jnp.stack(passage_outs, axis=0)
    final_rows = jnp.concatenate([query_outs[RELAY_SECTIONS - 1], passage_outs[RELAY_SECTIONS - 1]], axis=0)
    scaled = (final_rows.astype(jnp.float32) * final_gain.astype(jnp.float32)[None, :]).astype(jnp.bfloat16)
    projected = jnp.dot(scaled, w_vector, preferred_element_type=jnp.float32)
    vectors = (projected * lax.rsqrt(lax.optimization_barrier(jnp.sum(projected * projected, axis=1, keepdims=True)) + vector_epsilon)).astype(jnp.bfloat16)
    query_count = QUERIES * QLEN
    query_vectors = vectors[:query_count].reshape(QUERIES, QLEN, VEC)
    passage_vectors = vectors[query_count:].reshape(PASSAGES, PLEN, VEC)
    scores = late_scores(query_vectors, passage_vectors, lengths)
    divergence = divergence_rows(scores, teacher)
    return (boundary_queries, boundary_passages, scores, divergence)
```

```python
import jax
import jax.numpy as jnp
import numpy as np
from jax import lax
from jax.experimental import pallas as pl
from jax.experimental.pallas import tpu as pltpu
from jax.sharding import PartitionSpec as P

MODEL_WIDTH = 4096
HEAD_WIDTH = 128
VEC = 128
QLEN = 32
PLEN = 180


norm_epsilon = 1e-05
vector_epsilon = 1e-06
rope_base = 10000.0


def from_root(array, axis, root):
    mine = lax.axis_index(axis) == root
    return lax.psum(jnp.where(mine, array, jnp.zeros_like(array)), axis)


def rotate(values_in, positions):
    half_size = values_in.shape[-1] // 2
    frequency = rope_base ** (-jnp.arange(half_size).astype(jnp.float32) / half_size)
    angles = positions.astype(jnp.float32)[:, None] * frequency[None, :]
    cosine = jnp.cos(angles)[:, None, :]
    sine = jnp.sin(angles)[:, None, :]
    first_half = values_in[..., :half_size]
    second_half = values_in[..., half_size:]
    return jnp.concatenate(
        [first_half * cosine - second_half * sine, second_half * cosine + first_half * sine],
        axis=-1,
    )


def attend(queries, keys, values_in):
    batch_count, length, head_count, head_size = queries.shape
    key_heads = keys.shape[2]
    grouped = queries.reshape(batch_count, length, key_heads, head_count // key_heads, head_size)
    logits = jnp.einsum(
        "bskgd,bukd->bkgsu", grouped, keys, preferred_element_type=jnp.float32
    ) * head_size ** (-0.5)
    causal = jnp.arange(length)[:, None] >= jnp.arange(length)[None, :]
    weights = jnp.where(causal, jnp.exp(logits), 0.0)
    probability = (weights / jnp.sum(weights, axis=-1, keepdims=True)).astype(jnp.bfloat16)
    combined = jnp.einsum(
        "bkgsu,bukd->bskgd", probability, values_in, preferred_element_type=jnp.float32
    )
    return combined.reshape(batch_count * length, head_count * head_size).astype(jnp.bfloat16)


def by_sequence(array_in, head_number, seq_length):
    return array_in.reshape(-1, seq_length, head_number, HEAD_WIDTH)


def late_scores(query_vectors, passage_vectors, passage_lengths):
    sims = jnp.einsum(
        "qtc,psc->qtps", query_vectors, passage_vectors, preferred_element_type=jnp.float32
    )
    valid = jnp.arange(passage_vectors.shape[1])[None, :] < passage_lengths[:, None]
    masked = jnp.where(valid[None, None], sims, -3.0)
    return jnp.sum(jnp.max(masked, axis=3), axis=1)


def body(
    query_states,
    passage_hidden_states,
    w_query,
    key_matrix,
    value_matrix,
    w_out,
    final_gain,
    w_vector,
    lengths,
    teacher,
):
    query_rows = query_states[0]
    passage_rows = passage_hidden_states[0]
    query_count = query_rows.shape[0]
    joined = jnp.concatenate([query_rows, passage_rows], axis=0)
    widened = joined.astype(jnp.float32)
    squares = jnp.sum(widened * widened, axis=1)
    total = lax.psum(squares, "tensor")
    normed_local = (widened * lax.rsqrt(total / MODEL_WIDTH + norm_epsilon)[:, None]).astype(
        jnp.bfloat16
    )
    normed = lax.all_gather(normed_local, "tensor", axis=1, tiled=True)
    query_cols = w_query.shape[2]
    key_cols = key_matrix.shape[2]
    pieces = (
        lax.all_gather(w_query[0], "dp", axis=0, tiled=True),
        lax.all_gather(key_matrix[0], "dp", axis=0, tiled=True),
        lax.all_gather(value_matrix[0], "dp", axis=0, tiled=True),
    )
    queries, keys, unprojected_values = tuple(
        (jnp.dot(normed, piece, preferred_element_type=jnp.float32) for piece in pieces)
    )
    values_out = unprojected_values.astype(jnp.bfloat16)
    query_heads = query_cols // HEAD_WIDTH
    key_heads = key_cols // HEAD_WIDTH
    query_pos = jnp.arange(QLEN)
    passage_pos = jnp.arange(PLEN)
    short_q = rotate(by_sequence(queries[:query_count], query_heads, QLEN), query_pos).astype(
        jnp.bfloat16
    )
    short_k = rotate(by_sequence(keys[:query_count], key_heads, QLEN), query_pos).astype(
        jnp.bfloat16
    )
    short_v = by_sequence(values_out[:query_count], key_heads, QLEN)
    long_q = rotate(by_sequence(queries[query_count:], query_heads, PLEN), passage_pos).astype(
        jnp.bfloat16
    )
    long_k = rotate(by_sequence(keys[query_count:], key_heads, PLEN), passage_pos).astype(
        jnp.bfloat16
    )
    long_v = by_sequence(values_out[query_count:], key_heads, PLEN)
    attended = jnp.concatenate(
        [attend(short_q, short_k, short_v), attend(long_q, long_k, long_v)], axis=0
    )
    branch_full = jnp.dot(
        attended,
        lax.all_gather(w_out[0], "dp", axis=1, tiled=True),
        preferred_element_type=jnp.float32,
    )
    branch = lax.psum_scatter(
        branch_full.astype(jnp.bfloat16), "tensor", scatter_dimension=1, tiled=True
    ).astype(jnp.float32)
    updated = (widened + branch).astype(jnp.bfloat16)
    boundary_queries = updated[:query_count][None]
    boundary_passages = updated[query_count:][None]
    scaled = (updated.astype(jnp.float32) * final_gain.astype(jnp.float32)[None, :]).astype(
        jnp.bfloat16
    )
    partial_vec = jnp.dot(scaled, w_vector, preferred_element_type=jnp.float32)
    projected = lax.psum(partial_vec.astype(jnp.bfloat16), "tensor").astype(jnp.float32)
    vectors = (
        projected
        * lax.rsqrt(jnp.sum(projected * projected, axis=1, keepdims=True) + vector_epsilon)
    ).astype(jnp.bfloat16)
    query_vectors = vectors[:query_count].reshape(-1, QLEN, VEC)
    passage_vectors = vectors[query_count:].reshape(-1, PLEN, VEC)
    last_section = lax.axis_size("pipe") - 1
    query_vectors, passage_vectors = (
        from_root(query_vectors, "pipe", last_section),
        from_root(passage_vectors, "pipe", last_section),
    )
    owned = query_vectors.shape[0] // lax.axis_size("pipe")
    own_queries = lax.dynamic_slice_in_dim(query_vectors, lax.axis_index("pipe") * owned, owned, 0)
    pieces = (
        lax.all_gather(passage_vectors, "dp", axis=0, tiled=True),
        lax.all_gather(lengths, "dp", axis=0, tiled=True),
    )
    block = late_scores(own_queries, pieces[0], pieces[1])
    log_student = block - jnp.log(jnp.sum(jnp.exp(block), axis=1, keepdims=True))
    log_teacher = teacher - jnp.log(jnp.sum(jnp.exp(teacher), axis=1, keepdims=True))
    divergence = jnp.sum(jnp.exp(log_teacher) * (log_teacher - log_student), axis=1)
    return (boundary_queries, boundary_passages, block, divergence)


ROWS = 256
Q_ROWS = 64
MESH = pl.DeviceIdType.MESH


def remote(src, dst, send, recv, device):
    return pltpu.make_async_remote_copy(
        src_ref=src, dst_ref=dst, send_sem=send, recv_sem=recv, device_id=device, device_id_type=MESH
    )


def greet(devices):
    barrier = pltpu.get_barrier_semaphore()
    for device in devices:
        pl.semaphore_signal(barrier, inc=1, device_id=device, device_id_type=MESH)
    pl.semaphore_wait(barrier, len(devices))


def place():
    dp = lax.axis_index("dp")
    return dp // 2, lax.rem(dp, 2), lax.axis_index("tensor")


class Line:
    def __init__(self, own, held, send, recv, z, x):
        self.own, self.held, self.send_sem, self.recv_sem, self.z, self.x = own, held, send, recv, z, x

    def copies(self, step):
        z, x = self.z, self.x
        up_block = jnp.maximum(z - step, 0)
        down_block = jnp.minimum(z + step, 3)
        src_up = self.own if step == 0 else self.held(up_block)
        src_down = self.own if step == 0 else self.held(down_block)
        up = remote(
            src_up, self.held(up_block), self.send_sem.at[0, step], self.recv_sem.at[up_block],
            {"dp": jnp.minimum(z + 1, 3) * 2 + x},
        )
        down = remote(
            src_down, self.held(down_block), self.send_sem.at[1, step], self.recv_sem.at[down_block],
            {"dp": jnp.maximum(z - 1, 0) * 2 + x},
        )
        return ((z < 3) & (z >= step), up), ((z > 0) & (z + step <= 3), down)

    def send(self, step):
        for condition, copy in self.copies(step):
            pl.when(condition)(copy.start)

    def receive(self, step, then=None):
        for condition, block in ((self.z - 1 - step >= 0, self.z - 1 - step), (self.z + 1 + step <= 3, self.z + 1 + step)):

            @pl.when(condition)
            def _(block=block):
                ref = self.held(block)
                remote(ref, ref, self.send_sem.at[0, 0], self.recv_sem.at[block], {"dp": self.x}).wait_recv()
                if then is not None:
                    then(block)

    def finish(self):
        for step in range(3):
            for condition, copy in self.copies(step):
                pl.when(condition)(copy.wait_send)


def gather_kernel(
    x_ref, w_ref, wo_ref, xg, wg, wog,
    local_sem, line_send, line_recv, core_send, core_recv, w_send, w_recv, wx_send, wx_recv, wo_send, wo_recv,
):
    z, x, t = place()
    d = z * 2 + x
    side = {"dp": z * 2 + 1 - x}
    partner = {"tensor": 1 - t}
    others = [lax.rem(z + o, 4) for o in range(4)]
    greet([{"dp": others[o] * 2 + x} for o in (1, 2, 3)] + [side, partner])

    line = Line(x_ref, lambda b: xg.at[b, t], line_send, line_recv, z, x)

    def w_copy(o):
        return remote(w_ref.at[others[o]], wg.at[d], w_send.at[o], w_recv.at[o], {"dp": others[o] * 2 + x})

    def side_copy(o):
        origin = lax.rem(z + 4 - o, 4)
        slot = wg.at[origin * 2 + x]
        return remote(w_ref.at[z] if o == 0 else slot, slot, wx_send.at[o], wx_recv.at[o], side)

    def core_copy(block, own=False):
        slot = xg.at[block, t]
        return remote(x_ref if own else slot, slot, core_send.at[block], core_recv.at[block], partner)

    def w_receive(o):
        origin = lax.rem(z + 4 - o, 4)
        slot = wg.at[origin * 2 + x]
        remote(slot, slot, w_send.at[o], w_recv.at[o], side).wait_recv()
        side_copy(o).start()

    wo_copy = remote(wo_ref, wog.at[x], wo_send, wo_recv, side)
    side_copy(0).start()
    line.send(0)
    for o in (1, 3, 2):
        w_copy(o).start()
    core_copy(z, own=True).start()
    locals_ = [
        pltpu.make_async_copy(x_ref, xg.at[z, t], local_sem.at[0]),
        pltpu.make_async_copy(w_ref.at[z], wg.at[d], local_sem.at[1]),
        pltpu.make_async_copy(wo_ref, wog.at[x], local_sem.at[2]),
    ]
    for copy in locals_:
        copy.start()
    forward = lambda block: core_copy(block).start()
    line.receive(0, forward)
    line.send(1)
    w_receive(1)
    w_receive(3)
    wo_copy.start()
    line.receive(1, forward)
    line.send(2)
    w_receive(2)
    line.receive(2, forward)
    for o in range(4):
        origin = lax.rem(z + 4 - o, 4)
        slot = wg.at[origin * 2 + 1 - x]
        remote(slot, slot, wx_send.at[o], wx_recv.at[o], side).wait_recv()
    for block in range(4):
        slot = xg.at[block, 1 - t]
        remote(slot, slot, core_send.at[block], core_recv.at[block], partner).wait_recv()
    remote(wog.at[1 - x], wog.at[1 - x], wo_send, wo_recv, side).wait_recv()
    for copy in locals_:
        copy.wait()
    line.finish()
    for o in (1, 2, 3):
        w_copy(o).wait_send()
    for o in range(4):
        side_copy(o).wait_send()
        core_copy(o).wait_send()
    wo_copy.wait_send()


def gather(x_block, w_parts, w_out):
    dma = pltpu.SemaphoreType.DMA
    any_spec = pl.BlockSpec(memory_space=pl.ANY)
    return pl.pallas_call(
        gather_kernel,
        out_shape=(
            jax.ShapeDtypeStruct((4, 2) + x_block.shape, x_block.dtype),
            jax.ShapeDtypeStruct((8,) + w_parts.shape[1:], w_parts.dtype),
            jax.ShapeDtypeStruct((2,) + w_out.shape, w_out.dtype),
        ),
        in_specs=[any_spec] * 3,
        out_specs=(any_spec,) * 3,
        scratch_shapes=[
            dma((3,)), dma((2, 3)), dma((4,)), dma((4,)), dma((4,)),
            dma((4,)), dma((4,)), dma((4,)), dma((4,)), dma, dma,
        ],
        compiler_params=pltpu.CompilerParams(collective_id=1, has_side_effects=True),
        name="gather",
    )(x_block, w_parts, w_out)


def attention_kernel(x_ref, w_ref, cos_ref, sin_ref, out_ref):
    half = x_ref.shape[3]
    first, second = x_ref[0, 0], x_ref[0, 1]
    raw = jnp.dot(first, w_ref[:half], preferred_element_type=jnp.float32) + jnp.dot(
        second, w_ref[half:], preferred_element_type=jnp.float32
    )
    a, b = first.astype(jnp.float32), second.astype(jnp.float32)
    total = jnp.sum(a * a, axis=1, keepdims=True) + jnp.sum(b * b, axis=1, keepdims=True)
    raw = raw * lax.rsqrt(total / (2 * half) + norm_epsilon)
    cosine, sine = cos_ref[...], sin_ref[...]
    row = lax.broadcasted_iota(jnp.int32, (ROWS, ROWS), 0)
    col = lax.broadcasted_iota(jnp.int32, (ROWS, ROWS), 1)
    start = jnp.where(row < QLEN, 0, jnp.where(row < 2 * QLEN, QLEN, Q_ROWS))
    seen = (row >= col) & (col >= start)

    def turned(head):
        part = raw[:, head * HEAD_WIDTH : (head + 1) * HEAD_WIDTH]
        swapped = jnp.concatenate([part[:, HEAD_WIDTH // 2 :], part[:, : HEAD_WIDTH // 2]], axis=1)
        return (part * cosine + swapped * sine).astype(jnp.bfloat16)

    heads = raw.shape[1] // HEAD_WIDTH - 2
    key = turned(heads)
    value = raw[:, (heads + 1) * HEAD_WIDTH :].astype(jnp.bfloat16)
    for head in range(heads):
        logits = lax.dot_general(
            turned(head), key, (((1,), (1,)), ((), ())), preferred_element_type=jnp.float32
        ) * HEAD_WIDTH ** (-0.5)
        weights = jnp.where(seen, jnp.exp(logits), 0.0)
        probability = (weights / jnp.sum(weights, axis=1, keepdims=True)).astype(jnp.bfloat16)
        out_ref[0, :, head * HEAD_WIDTH : (head + 1) * HEAD_WIDTH] = jnp.dot(
            probability, value, preferred_element_type=jnp.float32
        ).astype(jnp.bfloat16)


def attention(xg, weights, cosine, sine):
    heads_cols = weights.shape[1] - 2 * HEAD_WIDTH
    return pl.pallas_call(
        attention_kernel,
        grid=(4,),
        out_shape=jax.ShapeDtypeStruct((4, ROWS, heads_cols), jnp.bfloat16),
        in_specs=[
            pl.BlockSpec((1,) + xg.shape[1:], lambda i: (i, 0, 0, 0)),
            pl.BlockSpec(weights.shape, lambda i: (0, 0)),
            pl.BlockSpec(cosine.shape, lambda i: (0, 0)),
            pl.BlockSpec(sine.shape, lambda i: (0, 0)),
        ],
        out_specs=pl.BlockSpec((1, ROWS, heads_cols), lambda i: (i, 0, 0)),
        compiler_params=pltpu.CompilerParams(vmem_limit_bytes=48 << 20),
        name="attention",
    )(xg, weights, cosine, sine)


def output_kernel(
    a_ref, wo_ref, x_ref, gain_ref, wv_ref, updated_ref, partial_ref,
    ag, term, other, total, branch,
    line_send, line_recv, core_send, core_recv, row_send, row_recv,
):
    z, x, t = place()
    partner = {"tensor": 1 - t}
    peers = [{"dp": lax.rem(z + o, 4) * 2 + x, "tensor": lax.rem(t + c, 2)} for o in range(4) for c in range(2)]
    greet(peers[1:])
    line = Line(a_ref, lambda b: ag.at[b], line_send, line_recv, z, x)
    line.send(0)
    ag[pl.ds(z, 1)] = a_ref[...][None]
    line.receive(0)
    line.send(1)
    line.receive(1)
    line.send(2)
    line.receive(2)

    half = ROWS // 2
    depth = a_ref.shape[2]
    cols = wo_ref.shape[2]
    group = z // 2
    parity = lax.rem(z, 2)

    def core_copy(o, rb):
        return remote(term.at[o, 1 - t], other.at[o], core_send.at[o], core_recv.at[o], partner)

    def row_copy(o, rb):
        return remote(
            total.at[o], branch.at[parity, t], row_send.at[o], row_recv.at[parity, t],
            {"dp": rb * 2 + x, "tensor": group},
        )

    blocks = [lax.rem(z + o, 4) for o in (1, 2, 3, 0)]
    for o, rb in enumerate(blocks):
        for side in range(2):
            acc = jnp.zeros((ROWS, cols), jnp.float32)
            for part in range(4):
                acc += jnp.dot(
                    ag[part, rb], wo_ref[side, part * depth : (part + 1) * depth],
                    preferred_element_type=jnp.float32,
                )
            rounded = acc.astype(jnp.bfloat16)
            term[o, 0, :, side * cols : (side + 1) * cols] = rounded[:half]
            term[o, 1, :, side * cols : (side + 1) * cols] = rounded[half:]
        core_copy(o, rb).start()
    mine = t == group
    for o, rb in enumerate(blocks):
        core_copy(o, rb).wait_recv()
        summed = term[o, t].astype(jnp.float32) + other[o].astype(jnp.float32)
        total[o] = summed.astype(jnp.bfloat16)
        if o < 3:
            row_copy(o, rb).start()
        else:
            pl.when(jnp.logical_not(mine))(row_copy(o, rb).start)

            @pl.when(mine)
            def _():
                branch[parity, t] = total[o]

    for p in range(2):
        for h in range(2):
            own_piece = mine & (parity == p) & (t == h)

            @pl.when(jnp.logical_not(own_piece))
            def _(p=p, h=h):
                slot = branch.at[p, h]
                remote(slot, slot, row_send.at[0], row_recv.at[p, h], partner).wait_recv()

    width = 2 * cols
    for h in range(2):
        rows = slice(h * half, (h + 1) * half)
        partial = jnp.zeros((half, VEC), jnp.float32)
        for p in range(2):
            columns = slice(p * width, (p + 1) * width)
            updated = (
                x_ref[rows, columns].astype(jnp.float32) + branch[p, h].astype(jnp.float32)
            ).astype(jnp.bfloat16)
            updated_ref[rows, columns] = updated
            scaled = (updated.astype(jnp.float32) * gain_ref[:, columns]).astype(jnp.bfloat16)
            partial += jnp.dot(scaled, wv_ref[columns], preferred_element_type=jnp.float32)
        partial_ref[rows] = partial.astype(jnp.bfloat16)
    line.finish()
    for o, rb in enumerate(blocks):
        core_copy(o, rb).wait_send()
        if o < 3:
            row_copy(o, rb).wait_send()
        else:
            pl.when(jnp.logical_not(mine))(row_copy(o, rb).wait_send)


def output(attended, wog, x_block, gain, w_vector):
    dma = pltpu.SemaphoreType.DMA
    bf16 = jnp.bfloat16
    cols = 2 * wog.shape[2]
    vmem = pl.BlockSpec(memory_space=pltpu.VMEM)
    return pl.pallas_call(
        output_kernel,
        out_shape=(
            jax.ShapeDtypeStruct(x_block.shape, bf16),
            jax.ShapeDtypeStruct((ROWS, VEC), bf16),
        ),
        in_specs=[vmem] * 5,
        out_specs=(vmem,) * 2,
        scratch_shapes=[
            pltpu.VMEM((4,) + attended.shape, bf16),
            pltpu.VMEM((4, 2, ROWS // 2, cols), bf16),
            pltpu.VMEM((4, ROWS // 2, cols), bf16),
            pltpu.VMEM((4, ROWS // 2, cols), bf16),
            pltpu.VMEM((2, 2, ROWS // 2, cols), bf16),
            dma((2, 3)), dma((4,)), dma((4,)), dma((4,)), dma((4,)), dma((2, 2)),
        ],
        compiler_params=pltpu.CompilerParams(
            collective_id=2, has_side_effects=True, vmem_limit_bytes=48 << 20
        ),
        name="output",
    )(attended, wog, x_block, gain, w_vector)


def vector_kernel(part_ref, valid_ref, all_ref, other, mine_buf, core_send, core_recv, send, recv):
    dp, pipe, t = lax.axis_index("dp"), lax.axis_index("pipe"), lax.axis_index("tensor")
    partner = {"tensor": 1 - t}
    ring = [lax.rem(dp + o, 8) for o in range(8)]
    pairs = [(o, p) for o in range(8) for p in range(2)][1:]
    targets = [{"dp": ring[o], "pipe": lax.rem(pipe + p, 2)} for o, p in pairs]
    greet([partner] + targets)
    exchange = remote(part_ref, other, core_send, core_recv, partner)
    exchange.start()
    exchange.wait_recv()
    projected = part_ref[...].astype(jnp.float32) + other[...].astype(jnp.float32)
    vectors = projected * lax.rsqrt(jnp.sum(projected * projected, axis=1, keepdims=True) + vector_epsilon)
    vectors = jnp.where(valid_ref[...] > 0.5, vectors, vectors[Q_ROWS : Q_ROWS + 1])
    mine_buf[...] = vectors.astype(jnp.bfloat16)

    def push(index):
        return remote(mine_buf, all_ref.at[dp], send.at[index], recv.at[dp], targets[index])

    @pl.when(pipe == 1)
    def _():
        for index in range(15):
            push(index).start()
        all_ref[pl.ds(dp, 1)] = mine_buf[...][None]

    for o in range(8):
        slot = all_ref.at[ring[o]]
        wait = remote(slot, slot, send.at[0], recv.at[ring[o]], partner).wait_recv
        if o == 0:
            pl.when(pipe == 0)(wait)
        else:
            wait()
    exchange.wait_send()

    @pl.when(pipe == 1)
    def _():
        for index in range(15):
            push(index).wait_send()


def share_vectors(partial, valid):
    dma = pltpu.SemaphoreType.DMA
    vmem = pl.BlockSpec(memory_space=pltpu.VMEM)
    return pl.pallas_call(
        vector_kernel,
        out_shape=jax.ShapeDtypeStruct((8, ROWS, VEC), jnp.bfloat16),
        in_specs=[vmem] * 2,
        out_specs=vmem,
        scratch_shapes=[
            pltpu.VMEM((ROWS, VEC), jnp.bfloat16),
            pltpu.VMEM((ROWS, VEC), jnp.bfloat16),
            dma, dma, dma((15,)), dma((8,)),
        ],
        compiler_params=pltpu.CompilerParams(collective_id=3, has_side_effects=True),
        name="share_vectors",
    )(partial, valid)


def rope_tables():
    position = np.concatenate([np.arange(QLEN), np.arange(QLEN), np.arange(ROWS - Q_ROWS)])
    half = HEAD_WIDTH // 2
    frequency = np.float32(rope_base) ** (-np.arange(half, dtype=np.float32) / np.float32(half))
    angles = position.astype(np.float32)[:, None] * frequency[None, :]
    cosine, sine = np.cos(angles), np.sin(angles)
    return (
        jnp.asarray(np.concatenate([cosine, cosine], axis=1), jnp.float32),
        jnp.asarray(np.concatenate([-sine, sine], axis=1), jnp.float32),
    )


def by_heads(
    query_states, passage_hidden_states, w_query, key_matrix, value_matrix, w_out,
    final_gain, w_vector, lengths, teacher,
):
    x_block = jnp.concatenate(
        [query_states[0], jnp.pad(passage_hidden_states[0], ((0, ROWS - Q_ROWS - PLEN), (0, 0)))], axis=0
    )
    depth = w_query.shape[1]
    w_parts = jnp.concatenate(
        [array[0].reshape(depth, 4, -1).transpose(1, 0, 2) for array in (w_query, key_matrix, value_matrix)],
        axis=2,
    )
    xg, wg, wog = gather(x_block, w_parts, w_out[0])
    cosine, sine = rope_tables()
    attended = attention(xg, wg.reshape(-1, wg.shape[2]), cosine, sine)
    updated, partial = output(
        attended, wog, x_block, final_gain.astype(jnp.float32)[None, :], w_vector
    )
    slot = jnp.arange(ROWS) - Q_ROWS
    valid = jnp.broadcast_to((slot < lengths[0])[:, None], (ROWS, VEC)).astype(jnp.float32)
    vectors = share_vectors(partial, valid)
    dp, pipe = lax.axis_index("dp"), lax.axis_index("pipe")
    own = lax.dynamic_slice(vectors, (dp, pipe * QLEN, 0), (1, QLEN, VEC))[0]
    sims = jnp.einsum("tc,psc->tps", own, vectors[:, Q_ROWS:], preferred_element_type=jnp.float32)
    block = jnp.sum(jnp.max(sims, axis=2), axis=0)[None]
    log_student = block - jnp.log(jnp.sum(jnp.exp(block), axis=1, keepdims=True))
    log_teacher = teacher - jnp.log(jnp.sum(jnp.exp(teacher), axis=1, keepdims=True))
    divergence = jnp.sum(jnp.exp(log_teacher) * (log_teacher - log_student), axis=1)
    return (
        updated[None, :Q_ROWS],
        updated[None, Q_ROWS : Q_ROWS + PLEN],
        block,
        divergence,
    )


def solution(mesh):
    in_specs = (
        P("pipe", "dp", "tensor"),
        P("pipe", "dp", "tensor"),
        P("pipe", "dp", "tensor"),
        P("pipe", "dp", "tensor"),
        P("pipe", "dp", "tensor"),
        P("pipe", "tensor", "dp"),
        P("tensor"),
        P("tensor", None),
        P("dp"),
        P(("dp", "pipe"), None),
    )
    out_specs = (
        P("pipe", "dp", "tensor"),
        P("pipe", "dp", "tensor"),
        P(("dp", "pipe"), None),
        P(("dp", "pipe")),
    )
    small = dict(mesh.shape) == {"dp": 8, "pipe": 2, "tensor": 2}
    return jax.shard_map(
        by_heads if small else body, mesh=mesh, in_specs=in_specs, out_specs=out_specs, check_vma=False
    )
```

```python
import jax
import jax.numpy as jnp
import numpy as np
from jax import lax
from jax.experimental import pallas as pl
from jax.experimental.pallas import tpu as pltpu
from jax.sharding import PartitionSpec as P

MODEL_WIDTH = 4096
HEAD_WIDTH = 128
VEC = 128
QLEN = 32
PLEN = 180


norm_epsilon = 1e-05
vector_epsilon = 1e-06
rope_base = 10000.0


def from_root(array, axis, root):
    mine = lax.axis_index(axis) == root
    return lax.psum(jnp.where(mine, array, jnp.zeros_like(array)), axis)


def rotate(values_in, positions):
    half_size = values_in.shape[-1] // 2
    frequency = rope_base ** (-jnp.arange(half_size).astype(jnp.float32) / half_size)
    angles = positions.astype(jnp.float32)[:, None] * frequency[None, :]
    cosine = jnp.cos(angles)[:, None, :]
    sine = jnp.sin(angles)[:, None, :]
    first_half = values_in[..., :half_size]
    second_half = values_in[..., half_size:]
    return jnp.concatenate(
        [first_half * cosine - second_half * sine, second_half * cosine + first_half * sine],
        axis=-1,
    )


def attend(queries, keys, values_in):
    batch_count, length, head_count, head_size = queries.shape
    key_heads = keys.shape[2]
    grouped = queries.reshape(batch_count, length, key_heads, head_count // key_heads, head_size)
    logits = jnp.einsum(
        "bskgd,bukd->bkgsu", grouped, keys, preferred_element_type=jnp.float32
    ) * head_size ** (-0.5)
    causal = jnp.arange(length)[:, None] >= jnp.arange(length)[None, :]
    weights = jnp.where(causal, jnp.exp(logits), 0.0)
    probability = (weights / jnp.sum(weights, axis=-1, keepdims=True)).astype(jnp.bfloat16)
    combined = jnp.einsum(
        "bkgsu,bukd->bskgd", probability, values_in, preferred_element_type=jnp.float32
    )
    return combined.reshape(batch_count * length, head_count * head_size).astype(jnp.bfloat16)


def by_sequence(array_in, head_number, seq_length):
    return array_in.reshape(-1, seq_length, head_number, HEAD_WIDTH)


def late_scores(query_vectors, passage_vectors, passage_lengths):
    sims = jnp.einsum(
        "qtc,psc->qtps", query_vectors, passage_vectors, preferred_element_type=jnp.float32
    )
    valid = jnp.arange(passage_vectors.shape[1])[None, :] < passage_lengths[:, None]
    masked = jnp.where(valid[None, None], sims, -3.0)
    return jnp.sum(jnp.max(masked, axis=3), axis=1)


def body(
    query_states,
    passage_hidden_states,
    w_query,
    key_matrix,
    value_matrix,
    w_out,
    final_gain,
    w_vector,
    lengths,
    teacher,
):
    query_rows = query_states[0]
    passage_rows = passage_hidden_states[0]
    query_count = query_rows.shape[0]
    joined = jnp.concatenate([query_rows, passage_rows], axis=0)
    widened = joined.astype(jnp.float32)
    squares = jnp.sum(widened * widened, axis=1)
    total = lax.psum(squares, "tensor")
    normed_local = (widened * lax.rsqrt(total / MODEL_WIDTH + norm_epsilon)[:, None]).astype(
        jnp.bfloat16
    )
    normed = lax.all_gather(normed_local, "tensor", axis=1, tiled=True)
    query_cols = w_query.shape[2]
    key_cols = key_matrix.shape[2]
    pieces = (
        lax.all_gather(w_query[0], "dp", axis=0, tiled=True),
        lax.all_gather(key_matrix[0], "dp", axis=0, tiled=True),
        lax.all_gather(value_matrix[0], "dp", axis=0, tiled=True),
    )
    queries, keys, unprojected_values = tuple(
        (jnp.dot(normed, piece, preferred_element_type=jnp.float32) for piece in pieces)
    )
    values_out = unprojected_values.astype(jnp.bfloat16)
    query_heads = query_cols // HEAD_WIDTH
    key_heads = key_cols // HEAD_WIDTH
    query_pos = jnp.arange(QLEN)
    passage_pos = jnp.arange(PLEN)
    short_q = rotate(by_sequence(queries[:query_count], query_heads, QLEN), query_pos).astype(
        jnp.bfloat16
    )
    short_k = rotate(by_sequence(keys[:query_count], key_heads, QLEN), query_pos).astype(
        jnp.bfloat16
    )
    short_v = by_sequence(values_out[:query_count], key_heads, QLEN)
    long_q = rotate(by_sequence(queries[query_count:], query_heads, PLEN), passage_pos).astype(
        jnp.bfloat16
    )
    long_k = rotate(by_sequence(keys[query_count:], key_heads, PLEN), passage_pos).astype(
        jnp.bfloat16
    )
    long_v = by_sequence(values_out[query_count:], key_heads, PLEN)
    attended = jnp.concatenate(
        [attend(short_q, short_k, short_v), attend(long_q, long_k, long_v)], axis=0
    )
    branch_full = jnp.dot(
        attended,
        lax.all_gather(w_out[0], "dp", axis=1, tiled=True),
        preferred_element_type=jnp.float32,
    )
    branch = lax.psum_scatter(
        branch_full.astype(jnp.bfloat16), "tensor", scatter_dimension=1, tiled=True
    ).astype(jnp.float32)
    updated = (widened + branch).astype(jnp.bfloat16)
    boundary_queries = updated[:query_count][None]
    boundary_passages = updated[query_count:][None]
    scaled = (updated.astype(jnp.float32) * final_gain.astype(jnp.float32)[None, :]).astype(
        jnp.bfloat16
    )
    partial_vec = jnp.dot(scaled, w_vector, preferred_element_type=jnp.float32)
    projected = lax.psum(partial_vec.astype(jnp.bfloat16), "tensor").astype(jnp.float32)
    vectors = (
        projected
        * lax.rsqrt(jnp.sum(projected * projected, axis=1, keepdims=True) + vector_epsilon)
    ).astype(jnp.bfloat16)
    query_vectors = vectors[:query_count].reshape(-1, QLEN, VEC)
    passage_vectors = vectors[query_count:].reshape(-1, PLEN, VEC)
    last_section = lax.axis_size("pipe") - 1
    query_vectors, passage_vectors = (
        from_root(query_vectors, "pipe", last_section),
        from_root(passage_vectors, "pipe", last_section),
    )
    owned = query_vectors.shape[0] // lax.axis_size("pipe")
    own_queries = lax.dynamic_slice_in_dim(query_vectors, lax.axis_index("pipe") * owned, owned, 0)
    pieces = (
        lax.all_gather(passage_vectors, "dp", axis=0, tiled=True),
        lax.all_gather(lengths, "dp", axis=0, tiled=True),
    )
    block = late_scores(own_queries, pieces[0], pieces[1])
    log_student = block - jnp.log(jnp.sum(jnp.exp(block), axis=1, keepdims=True))
    log_teacher = teacher - jnp.log(jnp.sum(jnp.exp(teacher), axis=1, keepdims=True))
    divergence = jnp.sum(jnp.exp(log_teacher) * (log_teacher - log_student), axis=1)
    return (boundary_queries, boundary_passages, block, divergence)


ROWS = 256
Q_ROWS = 64
MESH = pl.DeviceIdType.MESH


def remote(src, dst, send, recv, device):
    return pltpu.make_async_remote_copy(
        src_ref=src, dst_ref=dst, send_sem=send, recv_sem=recv, device_id=device, device_id_type=MESH
    )


def greet(devices):
    barrier = pltpu.get_barrier_semaphore()
    for device in devices:
        pl.semaphore_signal(barrier, inc=1, device_id=device, device_id_type=MESH)
    pl.semaphore_wait(barrier, len(devices))


def place():
    dp = lax.axis_index("dp")
    return dp // 2, lax.rem(dp, 2), lax.axis_index("tensor")


class Line:
    def __init__(self, own, held, send, recv, z, x):
        self.own, self.held, self.send_sem, self.recv_sem, self.z, self.x = own, held, send, recv, z, x

    def copies(self, step):
        z, x = self.z, self.x
        up_block = jnp.maximum(z - step, 0)
        down_block = jnp.minimum(z + step, 3)
        src_up = self.own if step == 0 else self.held(up_block)
        src_down = self.own if step == 0 else self.held(down_block)
        up = remote(
            src_up, self.held(up_block), self.send_sem.at[0, step], self.recv_sem.at[up_block],
            {"dp": jnp.minimum(z + 1, 3) * 2 + x},
        )
        down = remote(
            src_down, self.held(down_block), self.send_sem.at[1, step], self.recv_sem.at[down_block],
            {"dp": jnp.maximum(z - 1, 0) * 2 + x},
        )
        return ((z < 3) & (z >= step), up), ((z > 0) & (z + step <= 3), down)

    def send(self, step):
        for condition, copy in self.copies(step):
            pl.when(condition)(copy.start)

    def receive(self, step, then=None):
        for condition, block in ((self.z - 1 - step >= 0, self.z - 1 - step), (self.z + 1 + step <= 3, self.z + 1 + step)):

            @pl.when(condition)
            def _(block=block):
                ref = self.held(block)
                remote(ref, ref, self.send_sem.at[0, 0], self.recv_sem.at[block], {"dp": self.x}).wait_recv()
                if then is not None:
                    then(block)

    def finish(self):
        for step in range(3):
            for condition, copy in self.copies(step):
                pl.when(condition)(copy.wait_send)


def gather_kernel(
    x_ref, wq_ref, wk_ref, wv_ref, xg, wg,
    local_sem, line_send, line_recv, core_send, core_recv, w_send, w_recv, wx_send, wx_recv,
):
    z, x, t = place()
    d = z * 2 + x
    side = {"dp": z * 2 + 1 - x}
    partner = {"tensor": 1 - t}
    others = [lax.rem(z + o, 4) for o in range(4)]
    origins = [lax.rem(z + 4 - o, 4) for o in range(4)]
    greet([{"dp": others[o] * 2 + x} for o in (1, 2, 3)] + [side, partner])

    line = Line(x_ref, lambda b: xg.at[b, t], line_send, line_recv, z, x)
    sources = (wq_ref, wk_ref, wv_ref)
    widths = [ref.shape[1] // 4 for ref in sources]
    starts = [sum(widths[:i]) for i in range(3)]

    def part(i, owner):
        width = widths[i]
        return sources[i].at[:, pl.ds(pl.multiple_of(owner * width, width), width)]

    def slot_part(i, origin):
        return wg.at[origin, :, pl.ds(starts[i], widths[i])]

    def w_copy(o, i):
        return remote(
            part(i, others[o]), slot_part(i, d), w_send.at[o, i], w_recv.at[o, i], {"dp": others[o] * 2 + x}
        )

    def side_own(i):
        return remote(part(i, z), slot_part(i, d), wx_send.at[0, i], wx_recv.at[0, i], side)

    def side_copy(o):
        slot = wg.at[origins[o] * 2 + x]
        return remote(slot, slot, wx_send.at[o, 0], wx_recv.at[o, 0], side)

    def core_copy(block, own=False):
        slot = xg.at[block, t]
        return remote(x_ref if own else slot, slot, core_send.at[block], core_recv.at[block], partner)

    def w_receive(o):
        for i in range(3):
            slot = slot_part(i, origins[o] * 2 + x)
            remote(slot, slot, w_send.at[o, i], w_recv.at[o, i], side).wait_recv()
        side_copy(o).start()

    for o in (2, 1, 3):
        for i in range(3):
            w_copy(o, i).start()
    for i in range(3):
        side_own(i).start()
    line.send(0)
    core_copy(z, own=True).start()
    locals_ = [pltpu.make_async_copy(x_ref, xg.at[z, t], local_sem.at[0])] + [
        pltpu.make_async_copy(part(i, z), slot_part(i, d), local_sem.at[1 + i]) for i in range(3)
    ]
    for copy in locals_:
        copy.start()
    forward = lambda block: core_copy(block).start()
    line.receive(0, forward)
    line.send(1)
    w_receive(1)
    w_receive(3)
    w_receive(2)
    line.receive(1, forward)
    line.send(2)
    line.receive(2, forward)
    for i in range(3):
        slot = slot_part(i, z * 2 + 1 - x)
        remote(slot, slot, wx_send.at[0, i], wx_recv.at[0, i], side).wait_recv()
    for o in (1, 2, 3):
        slot = wg.at[origins[o] * 2 + 1 - x]
        remote(slot, slot, wx_send.at[o, 0], wx_recv.at[o, 0], side).wait_recv()
    for block in range(4):
        slot = xg.at[block, 1 - t]
        remote(slot, slot, core_send.at[block], core_recv.at[block], partner).wait_recv()
    for copy in locals_:
        copy.wait()
    line.finish()
    for o in (1, 2, 3):
        for i in range(3):
            w_copy(o, i).wait_send()
        side_copy(o).wait_send()
    for i in range(3):
        side_own(i).wait_send()
    for block in range(4):
        core_copy(block).wait_send()


def gather(x_block, w_query, key_matrix, value_matrix):
    dma = pltpu.SemaphoreType.DMA
    any_spec = pl.BlockSpec(memory_space=pl.ANY)
    columns = (w_query.shape[1] + key_matrix.shape[1] + value_matrix.shape[1]) // 4
    return pl.pallas_call(
        gather_kernel,
        out_shape=(
            jax.ShapeDtypeStruct((4, 2) + x_block.shape, x_block.dtype),
            jax.ShapeDtypeStruct((8, w_query.shape[0], columns), w_query.dtype),
        ),
        in_specs=[any_spec] * 4,
        out_specs=(any_spec,) * 2,
        scratch_shapes=[
            dma((4,)), dma((2, 3)), dma((4,)), dma((4,)), dma((4,)),
            dma((4, 3)), dma((4, 3)), dma((4, 3)), dma((4, 3)),
        ],
        compiler_params=pltpu.CompilerParams(collective_id=1, has_side_effects=True),
        name="gather",
    )(x_block, w_query, key_matrix, value_matrix)


def attention_kernel(x_ref, w_ref, cos_ref, sin_ref, out_ref):
    half = x_ref.shape[3]
    first, second = x_ref[0, 0], x_ref[0, 1]
    raw = jnp.dot(first, w_ref[:half], preferred_element_type=jnp.float32) + jnp.dot(
        second, w_ref[half:], preferred_element_type=jnp.float32
    )
    a, b = first.astype(jnp.float32), second.astype(jnp.float32)
    total = jnp.sum(a * a, axis=1, keepdims=True) + jnp.sum(b * b, axis=1, keepdims=True)
    raw = raw * lax.rsqrt(total / (2 * half) + norm_epsilon)
    cosine, sine = cos_ref[...], sin_ref[...]
    row = lax.broadcasted_iota(jnp.int32, (ROWS, ROWS), 0)
    col = lax.broadcasted_iota(jnp.int32, (ROWS, ROWS), 1)
    start = jnp.where(row < QLEN, 0, jnp.where(row < 2 * QLEN, QLEN, Q_ROWS))
    seen = (row >= col) & (col >= start)

    def turned(head):
        part = raw[:, head * HEAD_WIDTH : (head + 1) * HEAD_WIDTH]
        swapped = jnp.concatenate([part[:, HEAD_WIDTH // 2 :], part[:, : HEAD_WIDTH // 2]], axis=1)
        return (part * cosine + swapped * sine).astype(jnp.bfloat16)

    heads = raw.shape[1] // HEAD_WIDTH - 2
    key = turned(heads)
    value = raw[:, (heads + 1) * HEAD_WIDTH :].astype(jnp.bfloat16)
    for head in range(heads):
        logits = lax.dot_general(
            turned(head), key, (((1,), (1,)), ((), ())), preferred_element_type=jnp.float32
        ) * HEAD_WIDTH ** (-0.5)
        weights = jnp.where(seen, jnp.exp(logits), 0.0)
        probability = (weights / jnp.sum(weights, axis=1, keepdims=True)).astype(jnp.bfloat16)
        out_ref[0, :, head * HEAD_WIDTH : (head + 1) * HEAD_WIDTH] = jnp.dot(
            probability, value, preferred_element_type=jnp.float32
        ).astype(jnp.bfloat16)


def attention(xg, weights, cosine, sine):
    heads_cols = weights.shape[1] - 2 * HEAD_WIDTH
    return pl.pallas_call(
        attention_kernel,
        grid=(4,),
        out_shape=jax.ShapeDtypeStruct((4, ROWS, heads_cols), jnp.bfloat16),
        in_specs=[
            pl.BlockSpec((1,) + xg.shape[1:], lambda i: (i, 0, 0, 0)),
            pl.BlockSpec(weights.shape, lambda i: (0, 0)),
            pl.BlockSpec(cosine.shape, lambda i: (0, 0)),
            pl.BlockSpec(sine.shape, lambda i: (0, 0)),
        ],
        out_specs=pl.BlockSpec((1, ROWS, heads_cols), lambda i: (i, 0, 0)),
        compiler_params=pltpu.CompilerParams(vmem_limit_bytes=48 << 20),
        name="attention",
    )(xg, weights, cosine, sine)


def output_kernel(
    a_ref, wo_in, x_ref, gain_ref, wv_ref, updated_ref, partial_ref,
    ag, wog, term, other, total, branch, wo_sem, line_send, line_recv, core_send, core_recv, row_send, row_recv,
):
    z, x, t = place()
    partner = {"tensor": 1 - t}
    peers = [{"dp": lax.rem(z + o, 4) * 2 + x, "tensor": lax.rem(t + c, 2)} for o in range(4) for c in range(2)]
    side = {"dp": z * 2 + 1 - x}
    greet(peers[1:] + [side])
    lines = [
        Line(a_ref.at[rb], lambda b, rb=rb: ag.at[b, rb], line_send.at[rb], line_recv.at[rb], z, x)
        for rb in range(4)
    ]
    for line in lines:
        line.send(0)
    wo_copy = remote(wo_in, wog.at[x], wo_sem.at[0], wo_sem.at[1], side)
    wo_copy.start()
    wo_local = pltpu.make_async_copy(wo_in, wog.at[x], wo_sem.at[2])
    wo_local.start()
    ag[pl.ds(z, 1)] = a_ref[...][None]
    for step in (1, 2):
        for line in lines:
            line.receive(step - 1)
            line.send(step)
    wo_local.wait()
    remote(wog.at[1 - x], wog.at[1 - x], wo_sem.at[0], wo_sem.at[1], side).wait_recv()

    half = ROWS // 2
    depth = a_ref.shape[2]
    cols = wo_in.shape[1]
    group = z // 2
    parity = lax.rem(z, 2)

    def core_copy(o, rb):
        return remote(term.at[o, 1 - t], other.at[o], core_send.at[o], core_recv.at[o], partner)

    def row_copy(o, rb):
        return remote(
            total.at[o], branch.at[parity, t], row_send.at[o], row_recv.at[parity, t],
            {"dp": rb * 2 + x, "tensor": group},
        )

    blocks = [0, 1, 2, 3]
    mine = t == group

    def reduce(rb):
        core_copy(rb, rb).wait_recv()
        summed = term[rb, t].astype(jnp.float32) + other[rb].astype(jnp.float32)
        total[rb] = summed.astype(jnp.bfloat16)
        here = mine & (z == rb)
        pl.when(jnp.logical_not(here))(row_copy(rb, rb).start)

        @pl.when(here)
        def _():
            branch[parity, t] = total[rb]

    for rb in blocks:
        lines[rb].receive(2)
        for part_x in range(2):
            acc = jnp.zeros((ROWS, cols), jnp.float32)
            for part in range(4):
                acc += jnp.dot(
                    ag[part, rb], wog[part_x, part * depth : (part + 1) * depth],
                    preferred_element_type=jnp.float32,
                )
            rounded = acc.astype(jnp.bfloat16)
            term[rb, 0, :, part_x * cols : (part_x + 1) * cols] = rounded[:half]
            term[rb, 1, :, part_x * cols : (part_x + 1) * cols] = rounded[half:]
        core_copy(rb, rb).start()
        if rb > 0:
            reduce(rb - 1)
    reduce(3)

    for p in range(2):
        for h in range(2):
            own_piece = mine & (parity == p) & (t == h)

            @pl.when(jnp.logical_not(own_piece))
            def _(p=p, h=h):
                slot = branch.at[p, h]
                remote(slot, slot, row_send.at[0], row_recv.at[p, h], partner).wait_recv()

    width = 2 * cols
    for h in range(2):
        rows = slice(h * half, (h + 1) * half)
        partial = jnp.zeros((half, VEC), jnp.float32)
        for p in range(2):
            columns = slice(p * width, (p + 1) * width)
            updated = (
                x_ref[rows, columns].astype(jnp.float32) + branch[p, h].astype(jnp.float32)
            ).astype(jnp.bfloat16)
            updated_ref[rows, columns] = updated
            scaled = (updated.astype(jnp.float32) * gain_ref[:, columns]).astype(jnp.bfloat16)
            partial += jnp.dot(scaled, wv_ref[columns], preferred_element_type=jnp.float32)
        partial_ref[rows] = partial.astype(jnp.bfloat16)
    wo_copy.wait_send()
    for rb in blocks:
        lines[rb].finish()
        core_copy(rb, rb).wait_send()
        pl.when(jnp.logical_not(mine & (z == rb)))(row_copy(rb, rb).wait_send)


def output(attended, w_out, x_block, gain, w_vector):
    dma = pltpu.SemaphoreType.DMA
    bf16 = jnp.bfloat16
    cols = 2 * w_out.shape[1]
    vmem = pl.BlockSpec(memory_space=pltpu.VMEM)
    return pl.pallas_call(
        output_kernel,
        out_shape=(
            jax.ShapeDtypeStruct(x_block.shape, bf16),
            jax.ShapeDtypeStruct((ROWS, VEC), bf16),
        ),
        in_specs=[vmem, pl.BlockSpec(memory_space=pl.ANY), vmem, vmem, vmem],
        out_specs=(vmem,) * 2,
        scratch_shapes=[
            pltpu.VMEM((4,) + attended.shape, bf16),
            pltpu.VMEM((2,) + w_out.shape, bf16),
            pltpu.VMEM((4, 2, ROWS // 2, cols), bf16),
            pltpu.VMEM((4, ROWS // 2, cols), bf16),
            pltpu.VMEM((4, ROWS // 2, cols), bf16),
            pltpu.VMEM((2, 2, ROWS // 2, cols), bf16),
            dma((3,)), dma((4, 2, 3)), dma((4, 4)), dma((4,)), dma((4,)), dma((4,)), dma((2, 2)),
        ],
        compiler_params=pltpu.CompilerParams(
            collective_id=2, has_side_effects=True, vmem_limit_bytes=48 << 20
        ),
        name="output",
    )(attended, w_out, x_block, gain, w_vector)


def score_kernel(
    part_ref, length_ref, teacher_ref, score_ref, divergence_ref,
    other, vectors_buf, queries, mine, arrived, core_sem, q_send, q_recv, s_send, s_recv,
):
    dp, pipe, t = lax.axis_index("dp"), lax.axis_index("pipe"), lax.axis_index("tensor")
    partner = {"tensor": 1 - t}
    ring = [lax.rem(dp + o, 8) for o in range(8)]
    barrier = pltpu.get_barrier_semaphore()

    def signal(device):
        pl.semaphore_signal(barrier, inc=1, device_id=device, device_id_type=MESH)

    last = pipe == 1
    itself = last & (t == 1)
    signal(partner)
    for o in range(8):
        source = {"dp": ring[o], "pipe": 1, "tensor": pipe}
        if o == 0:
            pl.when(jnp.logical_not(itself))(lambda source=source: signal(source))
        else:
            signal(source)

    @pl.when(last)
    def _():
        for o in range(1, 8):
            signal({"dp": ring[o]})
        pl.semaphore_wait(barrier, 24 - t)

    @pl.when(jnp.logical_not(last))
    def _():
        pl.semaphore_wait(barrier, 1)

    exchange = remote(part_ref, other, core_sem.at[0], core_sem.at[1], partner)
    exchange.start()

    @pl.when(last)
    def _():
        exchange.wait_recv()
        projected = part_ref[...].astype(jnp.float32) + other[...].astype(jnp.float32)
        vectors = projected * lax.rsqrt(
            jnp.sum(projected * projected, axis=1, keepdims=True) + vector_epsilon
        )
        vectors_buf[...] = vectors.astype(jnp.bfloat16)
        own = pl.ds(pl.multiple_of(t * QLEN, QLEN), QLEN)

        def q_copy(o):
            return remote(
                vectors_buf.at[own], queries.at[dp], q_send.at[o], q_recv.at[dp], {"dp": ring[o]}
            )

        for o in range(1, 8):
            q_copy(o).start()
        queries[pl.ds(dp, 1)] = vectors_buf[own][None]
        passage = vectors_buf[Q_ROWS:]
        slot = lax.broadcasted_iota(jnp.int32, passage.shape, 0)
        passage = jnp.where(
            slot < length_ref[0], passage.astype(jnp.float32), passage[:1].astype(jnp.float32)
        ).astype(jnp.bfloat16)
        for o in range(1, 8):
            ref = queries.at[ring[o]]
            remote(ref, ref, q_send.at[o], q_recv.at[ring[o]], partner).wait_recv()
        sims = lax.dot_general(
            queries[...].reshape(8 * QLEN, VEC), passage, (((1,), (1,)), ((), ())),
            preferred_element_type=jnp.float32,
        )
        best = jnp.broadcast_to(jnp.max(sims, axis=1, keepdims=True), (8 * QLEN, VEC))
        mine[...] = jnp.sum(best.reshape(8, QLEN, VEC), axis=1)

        def s_copy(o, c):
            return remote(
                mine, arrived.at[dp], s_send.at[o, c], s_recv.at[dp],
                {"dp": ring[o], "pipe": t, "tensor": lax.rem(t + c, 2)},
            )

        first = s_copy(0, 0)
        pl.when(jnp.logical_not(itself))(first.start)

        @pl.when(itself)
        def _():
            arrived[pl.ds(dp, 1)] = mine[...][None]

        rest = [(o, c) for o in range(8) for c in range(2)][1:]
        for o, c in rest:
            s_copy(o, c).start()
        for o, c in rest:
            s_copy(o, c).wait_send()
        pl.when(jnp.logical_not(itself))(first.wait_send)
        for o in range(1, 8):
            q_copy(o).wait_send()

    @pl.when(jnp.logical_not(last))
    def _():
        exchange.wait_recv()

    exchange.wait_send()
    for o in range(8):
        ref = arrived.at[ring[o]]
        wait = remote(ref, ref, s_send.at[0, 0], s_recv.at[ring[o]], partner).wait_recv
        if o == 0:
            pl.when(jnp.logical_not(itself))(wait)
        else:
            wait()
    lane = lax.broadcasted_iota(jnp.int32, (1, VEC), 1)
    row = jnp.zeros((1, VEC), jnp.float32)
    for p in range(8):
        row = jnp.where(lane == p, arrived[p, pl.ds(dp, 1)], row)
    student = row[:, :8]
    score_ref[...] = student
    teacher = teacher_ref[...]
    log_student = student - jnp.log(jnp.sum(jnp.exp(student), axis=1, keepdims=True))
    log_teacher = teacher - jnp.log(jnp.sum(jnp.exp(teacher), axis=1, keepdims=True))
    divergence_ref[...] = jnp.sum(jnp.exp(log_teacher) * (log_teacher - log_student), axis=1, keepdims=True)


def score(partial, lengths, teacher):
    dma = pltpu.SemaphoreType.DMA
    vmem = pl.BlockSpec(memory_space=pltpu.VMEM)
    return pl.pallas_call(
        score_kernel,
        out_shape=(
            jax.ShapeDtypeStruct(teacher.shape, jnp.float32),
            jax.ShapeDtypeStruct((1, 1), jnp.float32),
        ),
        in_specs=[vmem, pl.BlockSpec(memory_space=pltpu.SMEM), vmem],
        out_specs=(vmem,) * 2,
        scratch_shapes=[
            pltpu.VMEM((ROWS, VEC), jnp.bfloat16),
            pltpu.VMEM((ROWS, VEC), jnp.bfloat16),
            pltpu.VMEM((8, QLEN, VEC), jnp.bfloat16),
            pltpu.VMEM((8, VEC), jnp.float32),
            pltpu.VMEM((8, 8, VEC), jnp.float32),
            dma((2,)), dma((8,)), dma((8,)), dma((8, 2)), dma((8,)),
        ],
        compiler_params=pltpu.CompilerParams(collective_id=3, has_side_effects=True),
        name="score",
    )(partial, lengths, teacher)


def rope_tables():
    position = np.concatenate([np.arange(QLEN), np.arange(QLEN), np.arange(ROWS - Q_ROWS)])
    half = HEAD_WIDTH // 2
    frequency = np.float32(rope_base) ** (-np.arange(half, dtype=np.float32) / np.float32(half))
    angles = position.astype(np.float32)[:, None] * frequency[None, :]
    cosine, sine = np.cos(angles), np.sin(angles)
    return (
        jnp.asarray(np.concatenate([cosine, cosine], axis=1), jnp.float32),
        jnp.asarray(np.concatenate([-sine, sine], axis=1), jnp.float32),
    )


def by_heads(
    query_states, passage_hidden_states, w_query, key_matrix, value_matrix, w_out,
    final_gain, w_vector, lengths, teacher,
):
    x_block = jnp.concatenate(
        [query_states[0], jnp.pad(passage_hidden_states[0], ((0, ROWS - Q_ROWS - PLEN), (0, 0)))], axis=0
    )
    xg, wg = gather(x_block, w_query[0], key_matrix[0], value_matrix[0])
    cosine, sine = rope_tables()
    attended = attention(xg, wg.reshape(-1, wg.shape[2]), cosine, sine)
    updated, partial = output(
        attended, w_out[0], x_block, final_gain.astype(jnp.float32)[None, :], w_vector
    )
    block, divergence = score(partial, lengths, teacher)
    return (
        updated[None, :Q_ROWS],
        updated[None, Q_ROWS : Q_ROWS + PLEN],
        block,
        divergence[0],
    )


def solution(mesh):
    in_specs = (
        P("pipe", "dp", "tensor"),
        P("pipe", "dp", "tensor"),
        P("pipe", "dp", "tensor"),
        P("pipe", "dp", "tensor"),
        P("pipe", "dp", "tensor"),
        P("pipe", "tensor", "dp"),
        P("tensor"),
        P("tensor", None),
        P("dp"),
        P(("dp", "pipe"), None),
    )
    out_specs = (
        P("pipe", "dp", "tensor"),
        P("pipe", "dp", "tensor"),
        P(("dp", "pipe"), None),
        P(("dp", "pipe")),
    )
    small = dict(mesh.shape) == {"dp": 8, "pipe": 2, "tensor": 2}
    return jax.shard_map(
        by_heads if small else body, mesh=mesh, in_specs=in_specs, out_specs=out_specs, check_vma=False
    )
```

```python
import jax
import jax.numpy as jnp
import numpy as np
from jax import lax
from jax.experimental import pallas as pl
from jax.experimental.pallas import tpu as pltpu
from jax.sharding import PartitionSpec as P

MODEL_WIDTH = 4096
HEAD_WIDTH = 128
VEC = 128
QLEN = 32
PLEN = 180


norm_epsilon = 1e-05
vector_epsilon = 1e-06
rope_base = 10000.0


def from_root(array, axis, root):
    mine = lax.axis_index(axis) == root
    return lax.psum(jnp.where(mine, array, jnp.zeros_like(array)), axis)


def rotate(values_in, positions):
    half_size = values_in.shape[-1] // 2
    frequency = rope_base ** (-jnp.arange(half_size).astype(jnp.float32) / half_size)
    angles = positions.astype(jnp.float32)[:, None] * frequency[None, :]
    cosine = jnp.cos(angles)[:, None, :]
    sine = jnp.sin(angles)[:, None, :]
    first_half = values_in[..., :half_size]
    second_half = values_in[..., half_size:]
    return jnp.concatenate(
        [first_half * cosine - second_half * sine, second_half * cosine + first_half * sine],
        axis=-1,
    )


def attend(queries, keys, values_in):
    batch_count, length, head_count, head_size = queries.shape
    key_heads = keys.shape[2]
    grouped = queries.reshape(batch_count, length, key_heads, head_count // key_heads, head_size)
    logits = jnp.einsum(
        "bskgd,bukd->bkgsu", grouped, keys, preferred_element_type=jnp.float32
    ) * head_size ** (-0.5)
    causal = jnp.arange(length)[:, None] >= jnp.arange(length)[None, :]
    weights = jnp.where(causal, jnp.exp(logits), 0.0)
    probability = (weights / jnp.sum(weights, axis=-1, keepdims=True)).astype(jnp.bfloat16)
    combined = jnp.einsum(
        "bkgsu,bukd->bskgd", probability, values_in, preferred_element_type=jnp.float32
    )
    return combined.reshape(batch_count * length, head_count * head_size).astype(jnp.bfloat16)


def by_sequence(array_in, head_number, seq_length):
    return array_in.reshape(-1, seq_length, head_number, HEAD_WIDTH)


def late_scores(query_vectors, passage_vectors, passage_lengths):
    sims = jnp.einsum(
        "qtc,psc->qtps", query_vectors, passage_vectors, preferred_element_type=jnp.float32
    )
    valid = jnp.arange(passage_vectors.shape[1])[None, :] < passage_lengths[:, None]
    masked = jnp.where(valid[None, None], sims, -3.0)
    return jnp.sum(jnp.max(masked, axis=3), axis=1)


def body(
    query_states,
    passage_hidden_states,
    w_query,
    key_matrix,
    value_matrix,
    w_out,
    final_gain,
    w_vector,
    lengths,
    teacher,
):
    query_rows = query_states[0]
    passage_rows = passage_hidden_states[0]
    query_count = query_rows.shape[0]
    joined = jnp.concatenate([query_rows, passage_rows], axis=0)
    widened = joined.astype(jnp.float32)
    squares = jnp.sum(widened * widened, axis=1)
    total = lax.psum(squares, "tensor")
    normed_local = (widened * lax.rsqrt(total / MODEL_WIDTH + norm_epsilon)[:, None]).astype(
        jnp.bfloat16
    )
    normed = lax.all_gather(normed_local, "tensor", axis=1, tiled=True)
    query_cols = w_query.shape[2]
    key_cols = key_matrix.shape[2]
    pieces = (
        lax.all_gather(w_query[0], "dp", axis=0, tiled=True),
        lax.all_gather(key_matrix[0], "dp", axis=0, tiled=True),
        lax.all_gather(value_matrix[0], "dp", axis=0, tiled=True),
    )
    queries, keys, unprojected_values = tuple(
        (jnp.dot(normed, piece, preferred_element_type=jnp.float32) for piece in pieces)
    )
    values_out = unprojected_values.astype(jnp.bfloat16)
    query_heads = query_cols // HEAD_WIDTH
    key_heads = key_cols // HEAD_WIDTH
    query_pos = jnp.arange(QLEN)
    passage_pos = jnp.arange(PLEN)
    short_q = rotate(by_sequence(queries[:query_count], query_heads, QLEN), query_pos).astype(
        jnp.bfloat16
    )
    short_k = rotate(by_sequence(keys[:query_count], key_heads, QLEN), query_pos).astype(
        jnp.bfloat16
    )
    short_v = by_sequence(values_out[:query_count], key_heads, QLEN)
    long_q = rotate(by_sequence(queries[query_count:], query_heads, PLEN), passage_pos).astype(
        jnp.bfloat16
    )
    long_k = rotate(by_sequence(keys[query_count:], key_heads, PLEN), passage_pos).astype(
        jnp.bfloat16
    )
    long_v = by_sequence(values_out[query_count:], key_heads, PLEN)
    attended = jnp.concatenate(
        [attend(short_q, short_k, short_v), attend(long_q, long_k, long_v)], axis=0
    )
    branch_full = jnp.dot(
        attended,
        lax.all_gather(w_out[0], "dp", axis=1, tiled=True),
        preferred_element_type=jnp.float32,
    )
    branch = lax.psum_scatter(
        branch_full.astype(jnp.bfloat16), "tensor", scatter_dimension=1, tiled=True
    ).astype(jnp.float32)
    updated = (widened + branch).astype(jnp.bfloat16)
    boundary_queries = updated[:query_count][None]
    boundary_passages = updated[query_count:][None]
    scaled = (updated.astype(jnp.float32) * final_gain.astype(jnp.float32)[None, :]).astype(
        jnp.bfloat16
    )
    partial_vec = jnp.dot(scaled, w_vector, preferred_element_type=jnp.float32)
    projected = lax.psum(partial_vec.astype(jnp.bfloat16), "tensor").astype(jnp.float32)
    vectors = (
        projected
        * lax.rsqrt(jnp.sum(projected * projected, axis=1, keepdims=True) + vector_epsilon)
    ).astype(jnp.bfloat16)
    query_vectors = vectors[:query_count].reshape(-1, QLEN, VEC)
    passage_vectors = vectors[query_count:].reshape(-1, PLEN, VEC)
    last_section = lax.axis_size("pipe") - 1
    query_vectors, passage_vectors = (
        from_root(query_vectors, "pipe", last_section),
        from_root(passage_vectors, "pipe", last_section),
    )
    owned = query_vectors.shape[0] // lax.axis_size("pipe")
    own_queries = lax.dynamic_slice_in_dim(query_vectors, lax.axis_index("pipe") * owned, owned, 0)
    pieces = (
        lax.all_gather(passage_vectors, "dp", axis=0, tiled=True),
        lax.all_gather(lengths, "dp", axis=0, tiled=True),
    )
    block = late_scores(own_queries, pieces[0], pieces[1])
    log_student = block - jnp.log(jnp.sum(jnp.exp(block), axis=1, keepdims=True))
    log_teacher = teacher - jnp.log(jnp.sum(jnp.exp(teacher), axis=1, keepdims=True))
    divergence = jnp.sum(jnp.exp(log_teacher) * (log_teacher - log_student), axis=1)
    return (boundary_queries, boundary_passages, block, divergence)


ROWS = 256
Q_ROWS = 64
MESH = pl.DeviceIdType.MESH


def remote(src, dst, send, recv, device):
    return pltpu.make_async_remote_copy(
        src_ref=src, dst_ref=dst, send_sem=send, recv_sem=recv, device_id=device, device_id_type=MESH
    )


def greet(devices):
    barrier = pltpu.get_barrier_semaphore()
    for device in devices:
        pl.semaphore_signal(barrier, inc=1, device_id=device, device_id_type=MESH)
    pl.semaphore_wait(barrier, len(devices))


def place():
    dp = lax.axis_index("dp")
    return dp // 2, lax.rem(dp, 2), lax.axis_index("tensor")


class Line:
    def __init__(self, own, held, send, recv, z, x):
        self.own, self.held, self.send_sem, self.recv_sem, self.z, self.x = own, held, send, recv, z, x

    def copies(self, step):
        z, x = self.z, self.x
        up_block = jnp.maximum(z - step, 0)
        down_block = jnp.minimum(z + step, 3)
        src_up = self.own if step == 0 else self.held(up_block)
        src_down = self.own if step == 0 else self.held(down_block)
        up = remote(
            src_up, self.held(up_block), self.send_sem.at[0, step], self.recv_sem.at[up_block],
            {"dp": jnp.minimum(z + 1, 3) * 2 + x},
        )
        down = remote(
            src_down, self.held(down_block), self.send_sem.at[1, step], self.recv_sem.at[down_block],
            {"dp": jnp.maximum(z - 1, 0) * 2 + x},
        )
        return ((z < 3) & (z >= step), up), ((z > 0) & (z + step <= 3), down)

    def send(self, step):
        for condition, copy in self.copies(step):
            pl.when(condition)(copy.start)

    def receive(self, step, then=None):
        for condition, block in ((self.z - 1 - step >= 0, self.z - 1 - step), (self.z + 1 + step <= 3, self.z + 1 + step)):

            @pl.when(condition)
            def _(block=block):
                ref = self.held(block)
                remote(ref, ref, self.send_sem.at[0, 0], self.recv_sem.at[block], {"dp": self.x}).wait_recv()
                if then is not None:
                    then(block)

    def finish(self):
        for step in range(3):
            for condition, copy in self.copies(step):
                pl.when(condition)(copy.wait_send)


def gather_kernel(
    x_ref, wq_ref, wk_ref, wv_ref, xg, wg,
    local_sem, line_send, line_recv, core_send, core_recv, w_send, w_recv, wx_send, wx_recv,
):
    z, x, t = place()
    d = z * 2 + x
    side = {"dp": z * 2 + 1 - x}
    partner = {"tensor": 1 - t}
    others = [lax.rem(z + o, 4) for o in range(4)]
    origins = [lax.rem(z + 4 - o, 4) for o in range(4)]
    greet([{"dp": others[o] * 2 + x} for o in (1, 2, 3)] + [side, partner])

    height = ROWS // 4
    cuts = [pl.ds(r * height, height) for r in range(4)]
    lines = [
        Line(x_ref.at[cut], lambda b, cut=cut: xg.at[b, t, cut], line_send.at[r], line_recv.at[r], z, x)
        for r, cut in enumerate(cuts)
    ]
    sources = (wq_ref, wk_ref, wv_ref)
    widths = [ref.shape[1] // 4 for ref in sources]
    starts = [sum(widths[:i]) for i in range(3)]

    def part(i, owner):
        width = widths[i]
        return sources[i].at[:, pl.ds(pl.multiple_of(owner * width, width), width)]

    def slot_part(i, origin):
        return wg.at[origin, :, pl.ds(starts[i], widths[i])]

    def w_copy(o, i):
        return remote(
            part(i, others[o]), slot_part(i, d), w_send.at[o, i], w_recv.at[o, i], {"dp": others[o] * 2 + x}
        )

    def side_own(i):
        return remote(part(i, z), slot_part(i, d), wx_send.at[0, i], wx_recv.at[0, i], side)

    def side_copy(o):
        slot = wg.at[origins[o] * 2 + x]
        return remote(slot, slot, wx_send.at[o, 0], wx_recv.at[o, 0], side)

    def core_copy(block, r, own=False):
        slot = xg.at[block, t, cuts[r]]
        source = x_ref.at[cuts[r]] if own else slot
        return remote(source, slot, core_send.at[block, r], core_recv.at[block, r], partner)

    def w_receive(o):
        for i in range(3):
            slot = slot_part(i, origins[o] * 2 + x)
            remote(slot, slot, w_send.at[o, i], w_recv.at[o, i], side).wait_recv()
        side_copy(o).start()

    for line in lines:
        line.send(0)
    for o in (2, 1, 3):
        for i in range(3):
            w_copy(o, i).start()
    for i in range(3):
        side_own(i).start()
    for r in range(4):
        core_copy(z, r, own=True).start()
    locals_ = [pltpu.make_async_copy(x_ref, xg.at[z, t], local_sem.at[0])] + [
        pltpu.make_async_copy(part(i, z), slot_part(i, d), local_sem.at[1 + i]) for i in range(3)
    ]
    for copy in locals_:
        copy.start()
    def advance(step):
        for r, line in enumerate(lines):
            line.receive(step, lambda block, r=r: core_copy(block, r).start())
            if step < 2:
                line.send(step + 1)

    advance(0)
    w_receive(1)
    w_receive(3)
    advance(1)
    w_receive(2)
    advance(2)
    for i in range(3):
        slot = slot_part(i, z * 2 + 1 - x)
        remote(slot, slot, wx_send.at[0, i], wx_recv.at[0, i], side).wait_recv()
    for o in (1, 2, 3):
        slot = wg.at[origins[o] * 2 + 1 - x]
        remote(slot, slot, wx_send.at[o, 0], wx_recv.at[o, 0], side).wait_recv()
    for block in range(4):
        for r in range(4):
            slot = xg.at[block, 1 - t, cuts[r]]
            remote(slot, slot, core_send.at[block, r], core_recv.at[block, r], partner).wait_recv()
    for copy in locals_:
        copy.wait()
    for line in lines:
        line.finish()
    for o in (1, 2, 3):
        for i in range(3):
            w_copy(o, i).wait_send()
        side_copy(o).wait_send()
    for i in range(3):
        side_own(i).wait_send()
    for block in range(4):
        for r in range(4):
            core_copy(block, r).wait_send()


def gather(x_block, w_query, key_matrix, value_matrix):
    dma = pltpu.SemaphoreType.DMA
    any_spec = pl.BlockSpec(memory_space=pl.ANY)
    columns = (w_query.shape[1] + key_matrix.shape[1] + value_matrix.shape[1]) // 4
    return pl.pallas_call(
        gather_kernel,
        out_shape=(
            jax.ShapeDtypeStruct((4, 2) + x_block.shape, x_block.dtype),
            jax.ShapeDtypeStruct((8, w_query.shape[0], columns), w_query.dtype),
        ),
        in_specs=[any_spec] * 4,
        out_specs=(any_spec,) * 2,
        scratch_shapes=[
            dma((4,)), dma((4, 2, 3)), dma((4, 4)), dma((4, 4)), dma((4, 4)),
            dma((4, 3)), dma((4, 3)), dma((4, 3)), dma((4, 3)),
        ],
        compiler_params=pltpu.CompilerParams(collective_id=1, has_side_effects=True),
        name="gather",
    )(x_block, w_query, key_matrix, value_matrix)


def attend_block(first, second, w_ref, cos_ref, sin_ref, store):
    half = first.shape[1]
    raw = jnp.dot(first, w_ref[:half], preferred_element_type=jnp.float32) + jnp.dot(
        second, w_ref[half:], preferred_element_type=jnp.float32
    )
    a, b = first.astype(jnp.float32), second.astype(jnp.float32)
    total = jnp.sum(a * a, axis=1, keepdims=True) + jnp.sum(b * b, axis=1, keepdims=True)
    raw = raw * lax.rsqrt(total / (2 * half) + norm_epsilon)
    cosine, sine = cos_ref[...], sin_ref[...]
    row = lax.broadcasted_iota(jnp.int32, (ROWS, ROWS), 0)
    col = lax.broadcasted_iota(jnp.int32, (ROWS, ROWS), 1)
    start = jnp.where(row < QLEN, 0, jnp.where(row < 2 * QLEN, QLEN, Q_ROWS))
    seen = (row >= col) & (col >= start)

    def turned(head):
        part = raw[:, head * HEAD_WIDTH : (head + 1) * HEAD_WIDTH]
        swapped = jnp.concatenate([part[:, HEAD_WIDTH // 2 :], part[:, : HEAD_WIDTH // 2]], axis=1)
        return (part * cosine + swapped * sine).astype(jnp.bfloat16)

    heads = raw.shape[1] // HEAD_WIDTH - 2
    key = turned(heads)
    value = raw[:, (heads + 1) * HEAD_WIDTH :].astype(jnp.bfloat16)
    for head in range(heads):
        logits = lax.dot_general(
            turned(head), key, (((1,), (1,)), ((), ())), preferred_element_type=jnp.float32
        ) * HEAD_WIDTH ** (-0.5)
        weights = jnp.where(seen, jnp.exp(logits), 0.0)
        probability = (weights / jnp.sum(weights, axis=1, keepdims=True)).astype(jnp.bfloat16)
        store(
            slice(head * HEAD_WIDTH, (head + 1) * HEAD_WIDTH),
            jnp.dot(probability, value, preferred_element_type=jnp.float32).astype(jnp.bfloat16),
        )


def output_kernel(
    xg, w_in, wo_in, cos_ref, sin_ref, x_ref, gain_ref, wv_ref, updated_ref, partial_ref,
    xs, w_all, load_sem, ag, wog, term, other, total, branch, wo_sem, line_send, line_recv, core_send, core_recv, row_send, row_recv,
):
    z, x, t = place()
    partner = {"tensor": 1 - t}
    peers = [{"dp": lax.rem(z + o, 4) * 2 + x, "tensor": lax.rem(t + c, 2)} for o in range(4) for c in range(2)]
    side = {"dp": z * 2 + 1 - x}
    load_w = pltpu.make_async_copy(w_in, w_all, load_sem.at[4])
    load_w.start()

    def load_x(rb):
        return pltpu.make_async_copy(xg.at[rb], xs.at[rb], load_sem.at[rb])

    for rb in range(4):
        load_x(rb).start()
    greet(peers[1:] + [side])
    wo_copy = remote(wo_in, wog.at[x], wo_sem.at[0], wo_sem.at[1], side)
    wo_copy.start()
    wo_local = pltpu.make_async_copy(wo_in, wog.at[x], wo_sem.at[2])
    wo_local.start()

    def line_of(rb):
        return Line(ag.at[z, rb], lambda b: ag.at[b, rb], line_send.at[rb], line_recv.at[rb], z, x)

    load_w.wait()

    @pl.loop(0, 4)
    def _(rb):
        load_x(rb).wait()

        def store(columns, values):
            ag[pl.ds(z, 1), pl.ds(rb, 1), :, columns] = values[None, None]

        attend_block(xs[rb, 0], xs[rb, 1], w_all, cos_ref, sin_ref, store)
        line_of(rb).send(0)

    lines = [line_of(rb) for rb in range(4)]
    for step in (1, 2):
        for line in lines:
            line.receive(step - 1)
            line.send(step)
    wo_local.wait()
    remote(wog.at[1 - x], wog.at[1 - x], wo_sem.at[0], wo_sem.at[1], side).wait_recv()

    half = ROWS // 2
    depth = ag.shape[3]
    cols = wo_in.shape[1]
    group = z // 2
    parity = lax.rem(z, 2)

    def core_copy(o, rb):
        return remote(term.at[o, 1 - t], other.at[o], core_send.at[o], core_recv.at[o], partner)

    def row_copy(o, rb):
        return remote(
            total.at[o], branch.at[parity, t], row_send.at[o], row_recv.at[parity, t],
            {"dp": rb * 2 + x, "tensor": group},
        )

    blocks = [0, 1, 2, 3]
    mine = t == group

    def reduce(rb):
        core_copy(rb, rb).wait_recv()
        summed = term[rb, t].astype(jnp.float32) + other[rb].astype(jnp.float32)
        total[rb] = summed.astype(jnp.bfloat16)
        here = mine & (z == rb)
        pl.when(jnp.logical_not(here))(row_copy(rb, rb).start)

        @pl.when(here)
        def _():
            branch[parity, t] = total[rb]

    for rb in blocks:
        lines[rb].receive(2)
        for part_x in range(2):
            acc = jnp.zeros((ROWS, cols), jnp.float32)
            for part in range(4):
                acc += jnp.dot(
                    ag[part, rb], wog[part_x, part * depth : (part + 1) * depth],
                    preferred_element_type=jnp.float32,
                )
            rounded = acc.astype(jnp.bfloat16)
            term[rb, 0, :, part_x * cols : (part_x + 1) * cols] = rounded[:half]
            term[rb, 1, :, part_x * cols : (part_x + 1) * cols] = rounded[half:]
        core_copy(rb, rb).start()
        if rb > 0:
            reduce(rb - 1)
    reduce(3)

    for p in range(2):
        for h in range(2):
            own_piece = mine & (parity == p) & (t == h)

            @pl.when(jnp.logical_not(own_piece))
            def _(p=p, h=h):
                slot = branch.at[p, h]
                remote(slot, slot, row_send.at[0], row_recv.at[p, h], partner).wait_recv()

    width = 2 * cols
    for h in range(2):
        rows = slice(h * half, (h + 1) * half)
        partial = jnp.zeros((half, VEC), jnp.float32)
        for p in range(2):
            columns = slice(p * width, (p + 1) * width)
            updated = (
                x_ref[rows, columns].astype(jnp.float32) + branch[p, h].astype(jnp.float32)
            ).astype(jnp.bfloat16)
            updated_ref[rows, columns] = updated
            scaled = (updated.astype(jnp.float32) * gain_ref[:, columns]).astype(jnp.bfloat16)
            partial += jnp.dot(scaled, wv_ref[columns], preferred_element_type=jnp.float32)
        partial_ref[rows] = partial.astype(jnp.bfloat16)
    wo_copy.wait_send()
    for rb in blocks:
        lines[rb].finish()
        core_copy(rb, rb).wait_send()
        pl.when(jnp.logical_not(mine & (z == rb)))(row_copy(rb, rb).wait_send)


def output(xg, weights, w_out, cosine, sine, x_block, gain, w_vector):
    dma = pltpu.SemaphoreType.DMA
    bf16 = jnp.bfloat16
    cols = 2 * w_out.shape[1]
    vmem = pl.BlockSpec(memory_space=pltpu.VMEM)
    return pl.pallas_call(
        output_kernel,
        out_shape=(
            jax.ShapeDtypeStruct(x_block.shape, bf16),
            jax.ShapeDtypeStruct((ROWS, VEC), bf16),
        ),
        in_specs=[pl.BlockSpec(memory_space=pl.ANY)] * 3 + [vmem] * 5,
        out_specs=(vmem,) * 2,
        scratch_shapes=[
            pltpu.VMEM(xg.shape, bf16),
            pltpu.VMEM(weights.shape, bf16),
            dma((5,)),
            pltpu.VMEM((4, 4, ROWS, weights.shape[1] - 2 * HEAD_WIDTH), bf16),
            pltpu.VMEM((2,) + w_out.shape, bf16),
            pltpu.VMEM((4, 2, ROWS // 2, cols), bf16),
            pltpu.VMEM((4, ROWS // 2, cols), bf16),
            pltpu.VMEM((4, ROWS // 2, cols), bf16),
            pltpu.VMEM((2, 2, ROWS // 2, cols), bf16),
            dma((3,)), dma((4, 2, 3)), dma((4, 4)), dma((4,)), dma((4,)), dma((4,)), dma((2, 2)),
        ],
        compiler_params=pltpu.CompilerParams(
            collective_id=2, has_side_effects=True, vmem_limit_bytes=48 << 20
        ),
        name="output",
    )(xg, weights, w_out, cosine, sine, x_block, gain, w_vector)


def score_kernel(
    part_ref, length_ref, teacher_ref, score_ref, divergence_ref,
    other, vectors_buf, queries, mine, arrived, core_sem, q_send, q_recv, s_send, s_recv,
):
    dp, pipe, t = lax.axis_index("dp"), lax.axis_index("pipe"), lax.axis_index("tensor")
    partner = {"tensor": 1 - t}
    ring = [lax.rem(dp + o, 8) for o in range(8)]
    barrier = pltpu.get_barrier_semaphore()

    def signal(device):
        pl.semaphore_signal(barrier, inc=1, device_id=device, device_id_type=MESH)

    last = pipe == 1
    itself = last & (t == 1)
    signal(partner)
    for o in range(8):
        source = {"dp": ring[o], "pipe": 1, "tensor": pipe}
        if o == 0:
            pl.when(jnp.logical_not(itself))(lambda source=source: signal(source))
        else:
            signal(source)

    @pl.when(last)
    def _():
        for o in range(1, 8):
            signal({"dp": ring[o]})
        pl.semaphore_wait(barrier, 24 - t)

    @pl.when(jnp.logical_not(last))
    def _():
        pl.semaphore_wait(barrier, 1)

    exchange = remote(part_ref, other, core_sem.at[0], core_sem.at[1], partner)
    exchange.start()

    @pl.when(last)
    def _():
        exchange.wait_recv()
        projected = part_ref[...].astype(jnp.float32) + other[...].astype(jnp.float32)
        vectors = projected * lax.rsqrt(
            jnp.sum(projected * projected, axis=1, keepdims=True) + vector_epsilon
        )
        vectors_buf[...] = vectors.astype(jnp.bfloat16)
        own = pl.ds(pl.multiple_of(t * QLEN, QLEN), QLEN)

        def q_copy(o):
            return remote(
                vectors_buf.at[own], queries.at[dp], q_send.at[o], q_recv.at[dp], {"dp": ring[o]}
            )

        for o in range(1, 8):
            q_copy(o).start()
        queries[pl.ds(dp, 1)] = vectors_buf[own][None]
        passage = vectors_buf[Q_ROWS:]
        slot = lax.broadcasted_iota(jnp.int32, passage.shape, 0)
        passage = jnp.where(
            slot < length_ref[0], passage.astype(jnp.float32), passage[:1].astype(jnp.float32)
        ).astype(jnp.bfloat16)
        for o in range(1, 8):
            ref = queries.at[ring[o]]
            remote(ref, ref, q_send.at[o], q_recv.at[ring[o]], partner).wait_recv()
        sims = lax.dot_general(
            queries[...].reshape(8 * QLEN, VEC), passage, (((1,), (1,)), ((), ())),
            preferred_element_type=jnp.float32,
        )
        best = jnp.broadcast_to(jnp.max(sims, axis=1, keepdims=True), (8 * QLEN, VEC))
        mine[...] = jnp.sum(best.reshape(8, QLEN, VEC), axis=1)

        def s_copy(o, c):
            return remote(
                mine, arrived.at[dp], s_send.at[o, c], s_recv.at[dp],
                {"dp": ring[o], "pipe": t, "tensor": lax.rem(t + c, 2)},
            )

        first = s_copy(0, 0)
        pl.when(jnp.logical_not(itself))(first.start)

        @pl.when(itself)
        def _():
            arrived[pl.ds(dp, 1)] = mine[...][None]

        rest = [(o, c) for o in range(8) for c in range(2)][1:]
        for o, c in rest:
            s_copy(o, c).start()
        for o, c in rest:
            s_copy(o, c).wait_send()
        pl.when(jnp.logical_not(itself))(first.wait_send)
        for o in range(1, 8):
            q_copy(o).wait_send()

    @pl.when(jnp.logical_not(last))
    def _():
        exchange.wait_recv()

    exchange.wait_send()
    for o in range(8):
        ref = arrived.at[ring[o]]
        wait = remote(ref, ref, s_send.at[0, 0], s_recv.at[ring[o]], partner).wait_recv
        if o == 0:
            pl.when(jnp.logical_not(itself))(wait)
        else:
            wait()
    lane = lax.broadcasted_iota(jnp.int32, (1, VEC), 1)
    row = jnp.zeros((1, VEC), jnp.float32)
    for p in range(8):
        row = jnp.where(lane == p, arrived[p, pl.ds(dp, 1)], row)
    student = row[:, :8]
    score_ref[...] = student
    teacher = teacher_ref[...]
    log_student = student - jnp.log(jnp.sum(jnp.exp(student), axis=1, keepdims=True))
    log_teacher = teacher - jnp.log(jnp.sum(jnp.exp(teacher), axis=1, keepdims=True))
    divergence_ref[...] = jnp.sum(jnp.exp(log_teacher) * (log_teacher - log_student), axis=1, keepdims=True)


def score(partial, lengths, teacher):
    dma = pltpu.SemaphoreType.DMA
    vmem = pl.BlockSpec(memory_space=pltpu.VMEM)
    return pl.pallas_call(
        score_kernel,
        out_shape=(
            jax.ShapeDtypeStruct(teacher.shape, jnp.float32),
            jax.ShapeDtypeStruct((1, 1), jnp.float32),
        ),
        in_specs=[vmem, pl.BlockSpec(memory_space=pltpu.SMEM), vmem],
        out_specs=(vmem,) * 2,
        scratch_shapes=[
            pltpu.VMEM((ROWS, VEC), jnp.bfloat16),
            pltpu.VMEM((ROWS, VEC), jnp.bfloat16),
            pltpu.VMEM((8, QLEN, VEC), jnp.bfloat16),
            pltpu.VMEM((8, VEC), jnp.float32),
            pltpu.VMEM((8, 8, VEC), jnp.float32),
            dma((2,)), dma((8,)), dma((8,)), dma((8, 2)), dma((8,)),
        ],
        compiler_params=pltpu.CompilerParams(collective_id=3, has_side_effects=True),
        name="score",
    )(partial, lengths, teacher)


def rope_tables():
    position = np.concatenate([np.arange(QLEN), np.arange(QLEN), np.arange(ROWS - Q_ROWS)])
    half = HEAD_WIDTH // 2
    frequency = np.float32(rope_base) ** (-np.arange(half, dtype=np.float32) / np.float32(half))
    angles = position.astype(np.float32)[:, None] * frequency[None, :]
    cosine, sine = np.cos(angles), np.sin(angles)
    return (
        jnp.asarray(np.concatenate([cosine, cosine], axis=1), jnp.float32),
        jnp.asarray(np.concatenate([-sine, sine], axis=1), jnp.float32),
    )


def by_heads(
    query_states, passage_hidden_states, w_query, key_matrix, value_matrix, w_out,
    final_gain, w_vector, lengths, teacher,
):
    x_block = jnp.concatenate(
        [query_states[0], jnp.pad(passage_hidden_states[0], ((0, ROWS - Q_ROWS - PLEN), (0, 0)))], axis=0
    )
    xg, wg = gather(x_block, w_query[0], key_matrix[0], value_matrix[0])
    cosine, sine = rope_tables()
    updated, partial = output(
        xg, wg.reshape(-1, wg.shape[2]), w_out[0], cosine, sine, x_block,
        final_gain.astype(jnp.float32)[None, :], w_vector,
    )
    block, divergence = score(partial, lengths, teacher)
    return (
        updated[None, :Q_ROWS],
        updated[None, Q_ROWS : Q_ROWS + PLEN],
        block,
        divergence[0],
    )


def solution(mesh):
    in_specs = (
        P("pipe", "dp", "tensor"),
        P("pipe", "dp", "tensor"),
        P("pipe", "dp", "tensor"),
        P("pipe", "dp", "tensor"),
        P("pipe", "dp", "tensor"),
        P("pipe", "tensor", "dp"),
        P("tensor"),
        P("tensor", None),
        P("dp"),
        P(("dp", "pipe"), None),
    )
    out_specs = (
        P("pipe", "dp", "tensor"),
        P("pipe", "dp", "tensor"),
        P(("dp", "pipe"), None),
        P(("dp", "pipe")),
    )
    small = dict(mesh.shape) == {"dp": 8, "pipe": 2, "tensor": 2}
    return jax.shard_map(
        by_heads if small else body, mesh=mesh, in_specs=in_specs, out_specs=out_specs, check_vma=False
    )
```

```python
import jax
import jax.numpy as jnp
import numpy as np
from jax import lax
from jax.experimental import pallas as pl
from jax.experimental.pallas import tpu as pltpu
from jax.sharding import PartitionSpec as P

MODEL_WIDTH = 4096
HEAD_WIDTH = 128
VEC = 128
QLEN = 32
PLEN = 180


norm_epsilon = 1e-05
vector_epsilon = 1e-06
rope_base = 10000.0


def from_root(array, axis, root):
    mine = lax.axis_index(axis) == root
    return lax.psum(jnp.where(mine, array, jnp.zeros_like(array)), axis)


def rotate(values_in, positions):
    half_size = values_in.shape[-1] // 2
    frequency = rope_base ** (-jnp.arange(half_size).astype(jnp.float32) / half_size)
    angles = positions.astype(jnp.float32)[:, None] * frequency[None, :]
    cosine = jnp.cos(angles)[:, None, :]
    sine = jnp.sin(angles)[:, None, :]
    first_half = values_in[..., :half_size]
    second_half = values_in[..., half_size:]
    return jnp.concatenate(
        [first_half * cosine - second_half * sine, second_half * cosine + first_half * sine],
        axis=-1,
    )


def attend(queries, keys, values_in):
    batch_count, length, head_count, head_size = queries.shape
    key_heads = keys.shape[2]
    grouped = queries.reshape(batch_count, length, key_heads, head_count // key_heads, head_size)
    logits = jnp.einsum(
        "bskgd,bukd->bkgsu", grouped, keys, preferred_element_type=jnp.float32
    ) * head_size ** (-0.5)
    causal = jnp.arange(length)[:, None] >= jnp.arange(length)[None, :]
    weights = jnp.where(causal, jnp.exp(logits), 0.0)
    probability = (weights / jnp.sum(weights, axis=-1, keepdims=True)).astype(jnp.bfloat16)
    combined = jnp.einsum(
        "bkgsu,bukd->bskgd", probability, values_in, preferred_element_type=jnp.float32
    )
    return combined.reshape(batch_count * length, head_count * head_size).astype(jnp.bfloat16)


def by_sequence(array_in, head_number, seq_length):
    return array_in.reshape(-1, seq_length, head_number, HEAD_WIDTH)


def late_scores(query_vectors, passage_vectors, passage_lengths):
    sims = jnp.einsum(
        "qtc,psc->qtps", query_vectors, passage_vectors, preferred_element_type=jnp.float32
    )
    valid = jnp.arange(passage_vectors.shape[1])[None, :] < passage_lengths[:, None]
    masked = jnp.where(valid[None, None], sims, -3.0)
    return jnp.sum(jnp.max(masked, axis=3), axis=1)


def body(
    query_states,
    passage_hidden_states,
    w_query,
    key_matrix,
    value_matrix,
    w_out,
    final_gain,
    w_vector,
    lengths,
    teacher,
):
    query_rows = query_states[0]
    passage_rows = passage_hidden_states[0]
    query_count = query_rows.shape[0]
    joined = jnp.concatenate([query_rows, passage_rows], axis=0)
    widened = joined.astype(jnp.float32)
    squares = jnp.sum(widened * widened, axis=1)
    total = lax.psum(squares, "tensor")
    normed_local = (widened * lax.rsqrt(total / MODEL_WIDTH + norm_epsilon)[:, None]).astype(
        jnp.bfloat16
    )
    normed = lax.all_gather(normed_local, "tensor", axis=1, tiled=True)
    query_cols = w_query.shape[2]
    key_cols = key_matrix.shape[2]
    pieces = (
        lax.all_gather(w_query[0], "dp", axis=0, tiled=True),
        lax.all_gather(key_matrix[0], "dp", axis=0, tiled=True),
        lax.all_gather(value_matrix[0], "dp", axis=0, tiled=True),
    )
    queries, keys, unprojected_values = tuple(
        (jnp.dot(normed, piece, preferred_element_type=jnp.float32) for piece in pieces)
    )
    values_out = unprojected_values.astype(jnp.bfloat16)
    query_heads = query_cols // HEAD_WIDTH
    key_heads = key_cols // HEAD_WIDTH
    query_pos = jnp.arange(QLEN)
    passage_pos = jnp.arange(PLEN)
    short_q = rotate(by_sequence(queries[:query_count], query_heads, QLEN), query_pos).astype(
        jnp.bfloat16
    )
    short_k = rotate(by_sequence(keys[:query_count], key_heads, QLEN), query_pos).astype(
        jnp.bfloat16
    )
    short_v = by_sequence(values_out[:query_count], key_heads, QLEN)
    long_q = rotate(by_sequence(queries[query_count:], query_heads, PLEN), passage_pos).astype(
        jnp.bfloat16
    )
    long_k = rotate(by_sequence(keys[query_count:], key_heads, PLEN), passage_pos).astype(
        jnp.bfloat16
    )
    long_v = by_sequence(values_out[query_count:], key_heads, PLEN)
    attended = jnp.concatenate(
        [attend(short_q, short_k, short_v), attend(long_q, long_k, long_v)], axis=0
    )
    branch_full = jnp.dot(
        attended,
        lax.all_gather(w_out[0], "dp", axis=1, tiled=True),
        preferred_element_type=jnp.float32,
    )
    branch = lax.psum_scatter(
        branch_full.astype(jnp.bfloat16), "tensor", scatter_dimension=1, tiled=True
    ).astype(jnp.float32)
    updated = (widened + branch).astype(jnp.bfloat16)
    boundary_queries = updated[:query_count][None]
    boundary_passages = updated[query_count:][None]
    scaled = (updated.astype(jnp.float32) * final_gain.astype(jnp.float32)[None, :]).astype(
        jnp.bfloat16
    )
    partial_vec = jnp.dot(scaled, w_vector, preferred_element_type=jnp.float32)
    projected = lax.psum(partial_vec.astype(jnp.bfloat16), "tensor").astype(jnp.float32)
    vectors = (
        projected
        * lax.rsqrt(jnp.sum(projected * projected, axis=1, keepdims=True) + vector_epsilon)
    ).astype(jnp.bfloat16)
    query_vectors = vectors[:query_count].reshape(-1, QLEN, VEC)
    passage_vectors = vectors[query_count:].reshape(-1, PLEN, VEC)
    last_section = lax.axis_size("pipe") - 1
    query_vectors, passage_vectors = (
        from_root(query_vectors, "pipe", last_section),
        from_root(passage_vectors, "pipe", last_section),
    )
    owned = query_vectors.shape[0] // lax.axis_size("pipe")
    own_queries = lax.dynamic_slice_in_dim(query_vectors, lax.axis_index("pipe") * owned, owned, 0)
    pieces = (
        lax.all_gather(passage_vectors, "dp", axis=0, tiled=True),
        lax.all_gather(lengths, "dp", axis=0, tiled=True),
    )
    block = late_scores(own_queries, pieces[0], pieces[1])
    log_student = block - jnp.log(jnp.sum(jnp.exp(block), axis=1, keepdims=True))
    log_teacher = teacher - jnp.log(jnp.sum(jnp.exp(teacher), axis=1, keepdims=True))
    divergence = jnp.sum(jnp.exp(log_teacher) * (log_teacher - log_student), axis=1)
    return (boundary_queries, boundary_passages, block, divergence)


ROWS = 256
Q_ROWS = 64
MESH = pl.DeviceIdType.MESH


def remote(src, dst, send, recv, device):
    return pltpu.make_async_remote_copy(
        src_ref=src, dst_ref=dst, send_sem=send, recv_sem=recv, device_id=device, device_id_type=MESH
    )


def greet(devices):
    barrier = pltpu.get_barrier_semaphore()
    for device in devices:
        pl.semaphore_signal(barrier, inc=1, device_id=device, device_id_type=MESH)
    pl.semaphore_wait(barrier, len(devices))


def place():
    dp = lax.axis_index("dp")
    return dp // 2, lax.rem(dp, 2), lax.axis_index("tensor")


class Line:
    def __init__(self, own, held, send, recv, z, x):
        self.own, self.held, self.send_sem, self.recv_sem, self.z, self.x = own, held, send, recv, z, x

    def copies(self, step):
        z, x = self.z, self.x
        up_block = jnp.maximum(z - step, 0)
        down_block = jnp.minimum(z + step, 3)
        src_up = self.own if step == 0 else self.held(up_block)
        src_down = self.own if step == 0 else self.held(down_block)
        up = remote(
            src_up, self.held(up_block), self.send_sem.at[0, step], self.recv_sem.at[up_block],
            {"dp": jnp.minimum(z + 1, 3) * 2 + x},
        )
        down = remote(
            src_down, self.held(down_block), self.send_sem.at[1, step], self.recv_sem.at[down_block],
            {"dp": jnp.maximum(z - 1, 0) * 2 + x},
        )
        return ((z < 3) & (z >= step), up), ((z > 0) & (z + step <= 3), down)

    def send(self, step):
        for condition, copy in self.copies(step):
            pl.when(condition)(copy.start)

    def receive(self, step, then=None):
        for condition, block in ((self.z - 1 - step >= 0, self.z - 1 - step), (self.z + 1 + step <= 3, self.z + 1 + step)):

            @pl.when(condition)
            def _(block=block):
                ref = self.held(block)
                remote(ref, ref, self.send_sem.at[0, 0], self.recv_sem.at[block], {"dp": self.x}).wait_recv()
                if then is not None:
                    then(block)

    def finish(self):
        for step in range(3):
            for condition, copy in self.copies(step):
                pl.when(condition)(copy.wait_send)


def gather_kernel(
    x_ref, wq_ref, wk_ref, wv_ref, xg, wg,
    local_sem, line_send, line_recv, core_send, core_recv, w_send, w_recv, wx_send, wx_recv,
):
    z, x, t = place()
    d = z * 2 + x
    side = {"dp": z * 2 + 1 - x}
    partner = {"tensor": 1 - t}
    others = [lax.rem(z + o, 4) for o in range(4)]
    origins = [lax.rem(z + 4 - o, 4) for o in range(4)]
    greet([{"dp": others[o] * 2 + x} for o in (1, 2, 3)] + [side, partner])

    height = ROWS // 4
    cuts = [pl.ds(r * height, height) for r in range(4)]
    lines = [
        Line(x_ref.at[cut], lambda b, cut=cut: xg.at[b, t, cut], line_send.at[r], line_recv.at[r], z, x)
        for r, cut in enumerate(cuts)
    ]
    sources = (wq_ref, wk_ref, wv_ref)
    widths = [ref.shape[1] // 4 for ref in sources]
    starts = [sum(widths[:i]) for i in range(3)]

    def part(i, owner):
        width = widths[i]
        return sources[i].at[:, pl.ds(pl.multiple_of(owner * width, width), width)]

    def slot_part(i, origin):
        return wg.at[origin, :, pl.ds(starts[i], widths[i])]

    def w_copy(o, i):
        return remote(
            part(i, others[o]), slot_part(i, d), w_send.at[o, i], w_recv.at[o, i], {"dp": others[o] * 2 + x}
        )

    def side_own(i):
        return remote(part(i, z), slot_part(i, d), wx_send.at[0, i], wx_recv.at[0, i], side)

    def side_copy(o):
        slot = wg.at[origins[o] * 2 + x]
        return remote(slot, slot, wx_send.at[o, 0], wx_recv.at[o, 0], side)

    def core_copy(block, r, own=False):
        slot = xg.at[block, t, cuts[r]]
        source = x_ref.at[cuts[r]] if own else slot
        return remote(source, slot, core_send.at[block, r], core_recv.at[block, r], partner)

    def w_receive(o):
        for i in range(3):
            slot = slot_part(i, origins[o] * 2 + x)
            remote(slot, slot, w_send.at[o, i], w_recv.at[o, i], side).wait_recv()
        side_copy(o).start()

    for line in lines:
        line.send(0)
    for o in (2, 1, 3):
        for i in range(3):
            w_copy(o, i).start()
    for i in range(3):
        side_own(i).start()
    for r in range(4):
        core_copy(z, r, own=True).start()
    locals_ = [pltpu.make_async_copy(x_ref, xg.at[z, t], local_sem.at[0])] + [
        pltpu.make_async_copy(part(i, z), slot_part(i, d), local_sem.at[1 + i]) for i in range(3)
    ]
    for copy in locals_:
        copy.start()
    def advance(step):
        for r, line in enumerate(lines):
            line.receive(step, lambda block, r=r: core_copy(block, r).start())
            if step < 2:
                line.send(step + 1)

    advance(0)
    w_receive(1)
    w_receive(3)
    advance(1)
    w_receive(2)
    advance(2)
    for i in range(3):
        slot = slot_part(i, z * 2 + 1 - x)
        remote(slot, slot, wx_send.at[0, i], wx_recv.at[0, i], side).wait_recv()
    for o in (1, 2, 3):
        slot = wg.at[origins[o] * 2 + 1 - x]
        remote(slot, slot, wx_send.at[o, 0], wx_recv.at[o, 0], side).wait_recv()
    for block in range(4):
        for r in range(4):
            slot = xg.at[block, 1 - t, cuts[r]]
            remote(slot, slot, core_send.at[block, r], core_recv.at[block, r], partner).wait_recv()
    for copy in locals_:
        copy.wait()
    for line in lines:
        line.finish()
    for o in (1, 2, 3):
        for i in range(3):
            w_copy(o, i).wait_send()
        side_copy(o).wait_send()
    for i in range(3):
        side_own(i).wait_send()
    for block in range(4):
        for r in range(4):
            core_copy(block, r).wait_send()


def gather(x_block, w_query, key_matrix, value_matrix):
    dma = pltpu.SemaphoreType.DMA
    any_spec = pl.BlockSpec(memory_space=pl.ANY)
    columns = (w_query.shape[1] + key_matrix.shape[1] + value_matrix.shape[1]) // 4
    return pl.pallas_call(
        gather_kernel,
        out_shape=(
            jax.ShapeDtypeStruct((4, 2) + x_block.shape, x_block.dtype),
            jax.ShapeDtypeStruct((8, w_query.shape[0], columns), w_query.dtype),
        ),
        in_specs=[any_spec] * 4,
        out_specs=(any_spec,) * 2,
        scratch_shapes=[
            dma((4,)), dma((4, 2, 3)), dma((4, 4)), dma((4, 4)), dma((4, 4)),
            dma((4, 3)), dma((4, 3)), dma((4, 3)), dma((4, 3)),
        ],
        compiler_params=pltpu.CompilerParams(collective_id=1, has_side_effects=True),
        name="gather",
    )(x_block, w_query, key_matrix, value_matrix)


def attend_block(first, second, w_ref, cos_ref, sin_ref, store):
    half = first.shape[1]
    raw = jnp.dot(first, w_ref[:half], preferred_element_type=jnp.float32) + jnp.dot(
        second, w_ref[half:], preferred_element_type=jnp.float32
    )
    a, b = first.astype(jnp.float32), second.astype(jnp.float32)
    total = jnp.sum(a * a, axis=1, keepdims=True) + jnp.sum(b * b, axis=1, keepdims=True)
    raw = raw * lax.rsqrt(total / (2 * half) + norm_epsilon)
    cosine, sine = cos_ref[...], sin_ref[...]
    row = lax.broadcasted_iota(jnp.int32, (ROWS, ROWS), 0)
    col = lax.broadcasted_iota(jnp.int32, (ROWS, ROWS), 1)
    start = jnp.where(row < QLEN, 0, jnp.where(row < 2 * QLEN, QLEN, Q_ROWS))
    seen = (row >= col) & (col >= start)

    def turned(head):
        part = raw[:, head * HEAD_WIDTH : (head + 1) * HEAD_WIDTH]
        swapped = jnp.concatenate([part[:, HEAD_WIDTH // 2 :], part[:, : HEAD_WIDTH // 2]], axis=1)
        return (part * cosine + swapped * sine).astype(jnp.bfloat16)

    heads = raw.shape[1] // HEAD_WIDTH - 2
    key = turned(heads)
    value = raw[:, (heads + 1) * HEAD_WIDTH :].astype(jnp.bfloat16)
    for head in range(heads):
        logits = lax.dot_general(
            turned(head), key, (((1,), (1,)), ((), ())), preferred_element_type=jnp.float32
        ) * HEAD_WIDTH ** (-0.5)
        weights = jnp.where(seen, jnp.exp(logits), 0.0)
        probability = (weights / jnp.sum(weights, axis=1, keepdims=True)).astype(jnp.bfloat16)
        store(
            slice(head * HEAD_WIDTH, (head + 1) * HEAD_WIDTH),
            jnp.dot(probability, value, preferred_element_type=jnp.float32).astype(jnp.bfloat16),
        )


def output_kernel(
    xg, w_in, wo_in, cos_ref, sin_ref, x_ref, gain_ref, wv_ref, updated_ref, partial_ref,
    xs, w_all, load_sem, ag, wog, term, other, total, branch, wo_sem, wo_send, wo_recv, line_send, line_recv, core_send, core_recv, row_send, row_recv,
):
    z, x, t = place()
    partner = {"tensor": 1 - t}
    peers = [{"dp": lax.rem(z + o, 4) * 2 + x, "tensor": lax.rem(t + c, 2)} for o in range(4) for c in range(2)]
    side = {"dp": z * 2 + 1 - x}
    load_w = pltpu.make_async_copy(w_in, w_all, load_sem.at[4])
    load_w.start()

    def load_x(rb):
        return pltpu.make_async_copy(xg.at[rb], xs.at[rb], load_sem.at[rb])

    for rb in range(4):
        load_x(rb).start()
    greet(peers[1:] + [side])
    wo_rows = wo_in.shape[0] // 8

    def wo_copy(k):
        cut = pl.ds(pl.multiple_of(k * wo_rows, wo_rows), wo_rows)
        return remote(wo_in.at[cut], wog.at[x, cut], wo_send.at[k], wo_recv.at[k], side)

    wo_local = pltpu.make_async_copy(wo_in, wog.at[x], wo_sem)
    wo_local.start()

    def line_of(rb):
        return Line(ag.at[z, rb], lambda b: ag.at[b, rb], line_send.at[rb], line_recv.at[rb], z, x)

    load_w.wait()

    @pl.loop(0, 4)
    def _(rb):
        load_x(rb).wait()

        def store(columns, values):
            ag[pl.ds(z, 1), pl.ds(rb, 1), :, columns] = values[None, None]

        attend_block(xs[rb, 0], xs[rb, 1], w_all, cos_ref, sin_ref, store)
        line_of(rb).send(0)
        wo_copy(rb).start()

    lines = [line_of(rb) for rb in range(4)]
    for step in (1, 2):
        for rb, line in enumerate(lines):
            line.receive(step - 1)
            line.send(step)
            if step == 1:
                wo_copy(4 + rb).start()
    wo_local.wait()
    for k in range(8):
        arriving = wog.at[1 - x, pl.ds(k * wo_rows, wo_rows)]
        remote(arriving, arriving, wo_send.at[k], wo_recv.at[k], side).wait_recv()

    half = ROWS // 2
    depth = ag.shape[3]
    cols = wo_in.shape[1]
    group = z // 2
    parity = lax.rem(z, 2)

    def core_copy(o, rb):
        return remote(term.at[o, 1 - t], other.at[o], core_send.at[o], core_recv.at[o], partner)

    def row_copy(o, rb):
        return remote(
            total.at[o], branch.at[parity, t], row_send.at[o], row_recv.at[parity, t],
            {"dp": rb * 2 + x, "tensor": group},
        )

    blocks = [0, 1, 2, 3]
    mine = t == group

    def reduce(rb):
        core_copy(rb, rb).wait_recv()
        summed = term[rb, t].astype(jnp.float32) + other[rb].astype(jnp.float32)
        total[rb] = summed.astype(jnp.bfloat16)
        here = mine & (z == rb)
        pl.when(jnp.logical_not(here))(row_copy(rb, rb).start)

        @pl.when(here)
        def _():
            branch[parity, t] = total[rb]

    for rb in blocks:
        lines[rb].receive(2)
        for part_x in range(2):
            acc = jnp.zeros((ROWS, cols), jnp.float32)
            for part in range(4):
                acc += jnp.dot(
                    ag[part, rb], wog[part_x, part * depth : (part + 1) * depth],
                    preferred_element_type=jnp.float32,
                )
            rounded = acc.astype(jnp.bfloat16)
            term[rb, 0, :, part_x * cols : (part_x + 1) * cols] = rounded[:half]
            term[rb, 1, :, part_x * cols : (part_x + 1) * cols] = rounded[half:]
        core_copy(rb, rb).start()
        if rb > 0:
            reduce(rb - 1)
    reduce(3)

    for p in range(2):
        for h in range(2):
            own_piece = mine & (parity == p) & (t == h)

            @pl.when(jnp.logical_not(own_piece))
            def _(p=p, h=h):
                slot = branch.at[p, h]
                remote(slot, slot, row_send.at[0], row_recv.at[p, h], partner).wait_recv()

    width = 2 * cols
    for h in range(2):
        rows = slice(h * half, (h + 1) * half)
        partial = jnp.zeros((half, VEC), jnp.float32)
        for p in range(2):
            columns = slice(p * width, (p + 1) * width)
            updated = (
                x_ref[rows, columns].astype(jnp.float32) + branch[p, h].astype(jnp.float32)
            ).astype(jnp.bfloat16)
            updated_ref[rows, columns] = updated
            scaled = (updated.astype(jnp.float32) * gain_ref[:, columns]).astype(jnp.bfloat16)
            partial += jnp.dot(scaled, wv_ref[columns], preferred_element_type=jnp.float32)
        partial_ref[rows] = partial.astype(jnp.bfloat16)
    for k in range(8):
        wo_copy(k).wait_send()
    for rb in blocks:
        lines[rb].finish()
        core_copy(rb, rb).wait_send()
        pl.when(jnp.logical_not(mine & (z == rb)))(row_copy(rb, rb).wait_send)


def output(xg, weights, w_out, cosine, sine, x_block, gain, w_vector):
    dma = pltpu.SemaphoreType.DMA
    bf16 = jnp.bfloat16
    cols = 2 * w_out.shape[1]
    vmem = pl.BlockSpec(memory_space=pltpu.VMEM)
    return pl.pallas_call(
        output_kernel,
        out_shape=(
            jax.ShapeDtypeStruct(x_block.shape, bf16),
            jax.ShapeDtypeStruct((ROWS, VEC), bf16),
        ),
        in_specs=[pl.BlockSpec(memory_space=pl.ANY)] * 3 + [vmem] * 5,
        out_specs=(vmem,) * 2,
        scratch_shapes=[
            pltpu.VMEM(xg.shape, bf16),
            pltpu.VMEM(weights.shape, bf16),
            dma((5,)),
            pltpu.VMEM((4, 4, ROWS, weights.shape[1] - 2 * HEAD_WIDTH), bf16),
            pltpu.VMEM((2,) + w_out.shape, bf16),
            pltpu.VMEM((4, 2, ROWS // 2, cols), bf16),
            pltpu.VMEM((4, ROWS // 2, cols), bf16),
            pltpu.VMEM((4, ROWS // 2, cols), bf16),
            pltpu.VMEM((2, 2, ROWS // 2, cols), bf16),
            dma, dma((8,)), dma((8,)), dma((4, 2, 3)), dma((4, 4)), dma((4,)), dma((4,)), dma((4,)), dma((2, 2)),
        ],
        compiler_params=pltpu.CompilerParams(
            collective_id=2, has_side_effects=True, vmem_limit_bytes=48 << 20
        ),
        name="output",
    )(xg, weights, w_out, cosine, sine, x_block, gain, w_vector)


def score_kernel(
    part_ref, length_ref, teacher_ref, score_ref, divergence_ref,
    other, vectors_buf, queries, mine, arrived, core_sem, q_send, q_recv, s_send, s_recv,
):
    dp, pipe, t = lax.axis_index("dp"), lax.axis_index("pipe"), lax.axis_index("tensor")
    partner = {"tensor": 1 - t}
    ring = [lax.rem(dp + o, 8) for o in range(8)]
    barrier = pltpu.get_barrier_semaphore()

    def signal(device):
        pl.semaphore_signal(barrier, inc=1, device_id=device, device_id_type=MESH)

    last = pipe == 1
    itself = last & (t == 1)
    signal(partner)
    for o in range(8):
        source = {"dp": ring[o], "pipe": 1, "tensor": pipe}
        if o == 0:
            pl.when(jnp.logical_not(itself))(lambda source=source: signal(source))
        else:
            signal(source)

    @pl.when(last)
    def _():
        for o in range(1, 8):
            signal({"dp": ring[o]})
        pl.semaphore_wait(barrier, 24 - t)

    @pl.when(jnp.logical_not(last))
    def _():
        pl.semaphore_wait(barrier, 1)

    exchange = remote(part_ref, other, core_sem.at[0], core_sem.at[1], partner)
    exchange.start()

    @pl.when(last)
    def _():
        exchange.wait_recv()
        projected = part_ref[...].astype(jnp.float32) + other[...].astype(jnp.float32)
        vectors = projected * lax.rsqrt(
            jnp.sum(projected * projected, axis=1, keepdims=True) + vector_epsilon
        )
        vectors_buf[...] = vectors.astype(jnp.bfloat16)
        own = pl.ds(pl.multiple_of(t * QLEN, QLEN), QLEN)

        def q_copy(o):
            return remote(
                vectors_buf.at[own], queries.at[dp], q_send.at[o], q_recv.at[dp], {"dp": ring[o]}
            )

        for o in range(1, 8):
            q_copy(o).start()
        queries[pl.ds(dp, 1)] = vectors_buf[own][None]
        passage = vectors_buf[Q_ROWS:]
        slot = lax.broadcasted_iota(jnp.int32, passage.shape, 0)
        passage = jnp.where(
            slot < length_ref[0], passage.astype(jnp.float32), passage[:1].astype(jnp.float32)
        ).astype(jnp.bfloat16)
        for o in range(1, 8):
            ref = queries.at[ring[o]]
            remote(ref, ref, q_send.at[o], q_recv.at[ring[o]], partner).wait_recv()
        sims = lax.dot_general(
            queries[...].reshape(8 * QLEN, VEC), passage, (((1,), (1,)), ((), ())),
            preferred_element_type=jnp.float32,
        )
        best = jnp.broadcast_to(jnp.max(sims, axis=1, keepdims=True), (8 * QLEN, VEC))
        mine[...] = jnp.sum(best.reshape(8, QLEN, VEC), axis=1)

        def s_copy(o, c):
            return remote(
                mine, arrived.at[dp], s_send.at[o, c], s_recv.at[dp],
                {"dp": ring[o], "pipe": t, "tensor": lax.rem(t + c, 2)},
            )

        first = s_copy(0, 0)
        pl.when(jnp.logical_not(itself))(first.start)

        @pl.when(itself)
        def _():
            arrived[pl.ds(dp, 1)] = mine[...][None]

        rest = [(o, c) for o in range(8) for c in range(2)][1:]
        for o, c in rest:
            s_copy(o, c).start()
        for o, c in rest:
            s_copy(o, c).wait_send()
        pl.when(jnp.logical_not(itself))(first.wait_send)
        for o in range(1, 8):
            q_copy(o).wait_send()

    @pl.when(jnp.logical_not(last))
    def _():
        exchange.wait_recv()

    exchange.wait_send()
    for o in range(8):
        ref = arrived.at[ring[o]]
        wait = remote(ref, ref, s_send.at[0, 0], s_recv.at[ring[o]], partner).wait_recv
        if o == 0:
            pl.when(jnp.logical_not(itself))(wait)
        else:
            wait()
    lane = lax.broadcasted_iota(jnp.int32, (1, VEC), 1)
    row = jnp.zeros((1, VEC), jnp.float32)
    for p in range(8):
        row = jnp.where(lane == p, arrived[p, pl.ds(dp, 1)], row)
    student = row[:, :8]
    score_ref[...] = student
    teacher = teacher_ref[...]
    log_student = student - jnp.log(jnp.sum(jnp.exp(student), axis=1, keepdims=True))
    log_teacher = teacher - jnp.log(jnp.sum(jnp.exp(teacher), axis=1, keepdims=True))
    divergence_ref[...] = jnp.sum(jnp.exp(log_teacher) * (log_teacher - log_student), axis=1, keepdims=True)


def score(partial, lengths, teacher):
    dma = pltpu.SemaphoreType.DMA
    vmem = pl.BlockSpec(memory_space=pltpu.VMEM)
    return pl.pallas_call(
        score_kernel,
        out_shape=(
            jax.ShapeDtypeStruct(teacher.shape, jnp.float32),
            jax.ShapeDtypeStruct((1, 1), jnp.float32),
        ),
        in_specs=[vmem, pl.BlockSpec(memory_space=pltpu.SMEM), vmem],
        out_specs=(vmem,) * 2,
        scratch_shapes=[
            pltpu.VMEM((ROWS, VEC), jnp.bfloat16),
            pltpu.VMEM((ROWS, VEC), jnp.bfloat16),
            pltpu.VMEM((8, QLEN, VEC), jnp.bfloat16),
            pltpu.VMEM((8, VEC), jnp.float32),
            pltpu.VMEM((8, 8, VEC), jnp.float32),
            dma((2,)), dma((8,)), dma((8,)), dma((8, 2)), dma((8,)),
        ],
        compiler_params=pltpu.CompilerParams(collective_id=3, has_side_effects=True),
        name="score",
    )(partial, lengths, teacher)


def rope_tables():
    position = np.concatenate([np.arange(QLEN), np.arange(QLEN), np.arange(ROWS - Q_ROWS)])
    half = HEAD_WIDTH // 2
    frequency = np.float32(rope_base) ** (-np.arange(half, dtype=np.float32) / np.float32(half))
    angles = position.astype(np.float32)[:, None] * frequency[None, :]
    cosine, sine = np.cos(angles), np.sin(angles)
    return (
        jnp.asarray(np.concatenate([cosine, cosine], axis=1), jnp.float32),
        jnp.asarray(np.concatenate([-sine, sine], axis=1), jnp.float32),
    )


def by_heads(
    query_states, passage_hidden_states, w_query, key_matrix, value_matrix, w_out,
    final_gain, w_vector, lengths, teacher,
):
    x_block = jnp.concatenate(
        [query_states[0], jnp.pad(passage_hidden_states[0], ((0, ROWS - Q_ROWS - PLEN), (0, 0)))], axis=0
    )
    xg, wg = gather(x_block, w_query[0], key_matrix[0], value_matrix[0])
    cosine, sine = rope_tables()
    updated, partial = output(
        xg, wg.reshape(-1, wg.shape[2]), w_out[0], cosine, sine, x_block,
        final_gain.astype(jnp.float32)[None, :], w_vector,
    )
    block, divergence = score(partial, lengths, teacher)
    return (
        updated[None, :Q_ROWS],
        updated[None, Q_ROWS : Q_ROWS + PLEN],
        block,
        divergence[0],
    )


def solution(mesh):
    in_specs = (
        P("pipe", "dp", "tensor"),
        P("pipe", "dp", "tensor"),
        P("pipe", "dp", "tensor"),
        P("pipe", "dp", "tensor"),
        P("pipe", "dp", "tensor"),
        P("pipe", "tensor", "dp"),
        P("tensor"),
        P("tensor", None),
        P("dp"),
        P(("dp", "pipe"), None),
    )
    out_specs = (
        P("pipe", "dp", "tensor"),
        P("pipe", "dp", "tensor"),
        P(("dp", "pipe"), None),
        P(("dp", "pipe")),
    )
    small = dict(mesh.shape) == {"dp": 8, "pipe": 2, "tensor": 2}
    return jax.shard_map(
        by_heads if small else body, mesh=mesh, in_specs=in_specs, out_specs=out_specs, check_vma=False
    )
```
